256 devices in a mesh: member: 32 (over z, x), tile: 8 (over y, core).
Axes of the slice: x: 4, y: 4, z: 8, core: 2. Of those that a mesh axis runs over, the one named last changes fastest.
Arguments:
- background: bfloat16 [256, 80, 64, 512], P('member', None, 'tile'), may hold values from -6 to 6
- obs_cell: int32 [32, 8, 256], P('member', 'tile'), may hold values from 0 to 127
- obs_channel: int32 [32, 8, 256], P('member', 'tile'), may hold values from 0 to 79
- obs_count: int32 [32, 8], P('member', 'tile'), may hold values from 1 to 256, as said below
- obs_value: float32 [32, 8, 256], P('member', 'tile'), may hold values from -8 to 8
- obs_precision: float32 [32, 8, 256], P('member', 'tile'), may hold values from 0.25 to 4
Outputs:
- analysis: bfloat16 [256, 80, 64, 512], P('member', None, 'tile')
The draws below stay inside these ranges and needn't reach their ends.
Inputs may be any that keep to these rules, and one draw needn't show every extreme that they name: obs_count is uneven across tiles; some tile has all 256 slots live.
All inputs are finite; a program needn't handle non-finite values.
Results may differ from the reference program's by a relative error of at most 0.0051.
Values may be sent and summed in bfloat16 or wider, within the bound.
No kernel may reach another device: no remote copies, remote signals or barrier semaphores. Data moves between devices by JAX's collectives and lax.ppermute only.
A program may use at most 192 MiB of HBM per device.

```python
import math
import jax
import jax.numpy as jnp
from jax import lax

K = 256
C = 80
LAT_DEV = 8
LON_DEV = 16
OBS_DEV = 256
PATCH_LAT = 4
NS_ITERS = 6
LOC = 8
BLOCKS = 32
BANDS = 8
NLAT = 64
NLON = 512


def draw_obs_count(key, part):
    key = jax.random.fold_in(key, 11)
    first_key, second_key, third_key = jax.random.split(key, 3)
    first = jax.random.randint(first_key, (BLOCKS, BANDS), 0, OBS_DEV)
    second = jax.random.randint(second_key, (BLOCKS, BANDS), 0, OBS_DEV)
    counts = OBS_DEV - first * second // (2 * OBS_DEV)
    chosen = jax.random.randint(third_key, (), 0, BLOCKS * BANDS)
    counts = counts.reshape(-1).at[chosen].set(OBS_DEV).reshape(BLOCKS, BANDS)
    return counts.astype(jnp.int32)


def with_ends(values, rng, low, largest):
    index_at = [jax.random.randint(jax.random.fold_in(rng, axis), (), 0, length) for axis, length in enumerate(values.shape)]
    main_axis = values.shape.index(max(values.shape))
    neighbour = index_at[:main_axis] + [(index_at[main_axis] + 1) % values.shape[main_axis]] + index_at[main_axis + 1:]
    return values.at[tuple(index_at)].set(low).at[tuple(neighbour)].set(largest)


def shard_levels(stream_key, shape, cuts, low, high):
    def one(dim, parts):
        steps = jax.random.uniform(jax.random.fold_in(jax.random.fold_in(stream_key, 6), dim), (parts,), jnp.float32, low / len(cuts), high / len(cuts))
        return jnp.repeat(jnp.exp(steps), shape[dim] // parts).reshape((-1,) + (1,) * (len(shape) - dim - 1))

    level = one(*cuts[0])
    for cut in cuts[1:]:
        level = level * one(*cut)
    return level


def centred(own_key, extent, scale, reach, shards=(), held_as=jnp.bfloat16):
    factor_of = shard_levels(own_key, extent, shards, -0.22, 0.18) if shards else 1.0
    values = jax.random.normal(own_key, extent, jnp.float32) * scale * factor_of
    return jnp.minimum(jnp.maximum(values, -reach), reach).astype(held_as)


def setup_inputs(seed: int = 0) -> dict:
    streams_of = jax.random.split(jax.random.key(seed), 7)
    return {
        "background": centred(streams_of[0], (K, C, NLAT, NLON), 1.0, 6.0, ((0, 32), (2, 8))),
        "obs_cell": with_ends(jax.random.randint(streams_of[1], (BLOCKS, BANDS, OBS_DEV), 0, LAT_DEV * LON_DEV), jax.random.fold_in(streams_of[1], 1), 0, (LAT_DEV * LON_DEV) - 1).astype(jnp.int32),
        "obs_channel": with_ends(jax.random.randint(streams_of[2], (BLOCKS, BANDS, OBS_DEV), 0, C), jax.random.fold_in(streams_of[2], 1), 0, C - 1).astype(jnp.int32),
        "obs_count": draw_obs_count(jax.random.fold_in(streams_of[6], 71), 0),
        "obs_value": centred(streams_of[4], (BLOCKS, BANDS, OBS_DEV), 1.5, 8.0, ((0, 32), (1, 8)), jnp.float32),
        "obs_precision": jnp.clip(jnp.exp(math.log(4.0) - 2.7725887 * jax.random.uniform(streams_of[5], (BLOCKS, BANDS, OBS_DEV), jnp.float32) ** shard_levels(streams_of[5], (BLOCKS, BANDS, OBS_DEV), ((0, 32), (1, 8)), -0.2, 0.2)), 0.25, 4.0),
    }


def obs_pack(values, obs_value, obs_precision, obs_count, obs_cell):
    members = values.astype(jnp.float32)
    centre = lax.optimization_barrier(jnp.mean(members, axis=0))
    anomaly = members - centre[None]
    departure = obs_value - centre
    slot_index = jnp.arange(values.shape[1], dtype=jnp.int32)
    inside = (slot_index < obs_count).astype(jnp.float32)
    weight = inside * obs_precision / (values.shape[0] - 1.0)
    row_pos = (obs_cell // LON_DEV).astype(jnp.float32)
    col_pos = (obs_cell % LON_DEV).astype(jnp.float32)
    return jnp.concatenate([anomaly, departure[None], weight[None], row_pos[None], col_pos[None]], 0)

def tile_weights(nearby):
    members = nearby.shape[2] - 4
    highest = lax.Precision.HIGHEST
    shifts = jnp.arange(3, dtype=jnp.float32) - 1.0
    lat_pos = nearby[:, :, members + 2, :] + (shifts * LAT_DEV)[None, :, None]
    lon_pos = nearby[:, :, members + 3, :] + (shifts * LON_DEV)[:, None, None]
    patch_count = LAT_DEV // PATCH_LAT
    lat_centre = jnp.arange(patch_count, dtype=jnp.float32) * PATCH_LAT + (PATCH_LAT - 1) / 2.0
    lon_centre = (LON_DEV - 1) / 2.0
    dist = (lat_pos[None] - lat_centre[:, None, None, None]) ** 2 + (lon_pos[None] - lon_centre) ** 2
    taper = jnp.exp(-dist / (2.0 * LOC * LOC))
    obs_weight = (taper * nearby[:, :, members + 1, :][None]).reshape(patch_count, -1)
    anomaly = nearby[:, :, :members, :].transpose(2, 0, 1, 3).reshape(members, -1)
    departure = nearby[:, :, members, :].reshape(-1)
    gram = jnp.einsum('ko,po,jo->pkj', anomaly, obs_weight, anomaly, precision=highest)
    drive = jnp.einsum('ko,po->pk', anomaly, obs_weight * departure[None], precision=highest)
    identity = jnp.eye(members, dtype=jnp.float32)
    system = identity[None] + gram
    scale = jnp.sqrt(lax.optimization_barrier(jnp.sum(system * system, axis=(1, 2))))
    root = system / scale[:, None, None]
    inverse = jnp.broadcast_to(identity, system.shape)
    for sweep_index in range(NS_ITERS):
        factor = 1.5 * identity - 0.5 * jnp.matmul(inverse, root, precision=highest)
        root = jnp.matmul(root, factor, precision=highest)
        inverse = jnp.matmul(factor, inverse, precision=highest)
    spread = inverse / jnp.sqrt(scale)[:, None, None]
    partial_w = jnp.einsum('pjk,pk->pj', spread, drive, precision=highest)
    shift = jnp.einsum('pjk,pk->pj', spread, partial_w, precision=highest)
    weights = (spread + shift[:, :, None]).astype(jnp.bfloat16)
    colsum = lax.optimization_barrier(jnp.sum(weights.astype(jnp.float32), axis=1))
    return (weights, colsum)

def transform(states, weights, colsum):
    members, chans = (states.shape[0], states.shape[1])
    patch_count = weights.shape[0]
    mean_state = lax.optimization_barrier(jnp.sum(states.astype(jnp.float32), axis=0)) / members
    blocked = states.reshape(members, chans, patch_count, PATCH_LAT, LON_DEV).astype(jnp.float32)
    mixed = jnp.einsum('jcpis,pjk->kcpis', blocked, weights.astype(jnp.float32))
    mean_block = mean_state.reshape(chans, patch_count, PATCH_LAT, LON_DEV)
    keep = (1.0 - colsum).transpose(1, 0)[:, None, :, None, None]
    result = mixed + mean_block[None] * keep
    return result.astype(jnp.bfloat16).reshape(states.shape)

def reference(background, obs_cell, obs_channel, obs_count, obs_value, obs_precision):
    lat_index = (jnp.arange(BANDS, dtype=jnp.int32) * LAT_DEV)[None, :, None] + obs_cell // LON_DEV
    lon_index = (jnp.arange(BLOCKS, dtype=jnp.int32) * LON_DEV)[:, None, None] + obs_cell % LON_DEV
    values = background[:, obs_channel, lat_index, lon_index]
    inner = jax.vmap(obs_pack, in_axes=(1, 0, 0, 0, 0))
    packs = jax.vmap(inner, in_axes=(1, 0, 0, 0, 0))(values, obs_value, obs_precision, obs_count, obs_cell)
    padded = jnp.pad(packs, ((0, 0), (1, 1), (0, 0), (0, 0)))
    padded = jnp.concatenate([padded[-1:], padded, padded[:1]], 0)

    def one_tile(flat):
        block = (flat // BANDS).astype(jnp.int32)
        band = (flat % BANDS).astype(jnp.int32)
        zero = jnp.zeros((), jnp.int32)
        nearby = lax.dynamic_slice(padded, (block, band, zero, zero), (3, 3, K + 4, OBS_DEV))
        states = lax.dynamic_slice(background, (zero, zero, band * LAT_DEV, block * LON_DEV), (K, C, LAT_DEV, LON_DEV))
        weights, colsum = tile_weights(nearby)
        return transform(states, weights, colsum)
    tiles = lax.map(one_tile, jnp.arange(BLOCKS * BANDS, dtype=jnp.int32))
    tiles = tiles.reshape(BLOCKS, BANDS, K, C, LAT_DEV, LON_DEV).transpose(2, 3, 1, 4, 0, 5)
    return tiles.reshape(K, C, NLAT, NLON)
```

```python
import functools

import jax
import jax.numpy as jnp
from jax import lax
from jax.experimental import pallas as pl
from jax.experimental.pallas import tpu as pltpu
from jax.sharding import PartitionSpec as P

LAT_DEV = 8
LON_DEV = 16
PATCH_LAT = 4
NS_ITERS = 6
LOC = 8
MEM_DEV = 8
LANES = 128
CHUNKS = (20, 20)
NT = (((1,), (1,)), ((), ()))
NN = (((1,), (0,)), ((), ()))
VMEM_LIMIT = 48 * 1024 * 1024


def swap_groups(parts, sign):
    lane_group = lax.broadcasted_iota(jnp.int32, parts[0].shape, 1) // LON_DEV
    parts = list(parts)
    for step in (4, 2, 1):
        low = (lane_group & step) == 0
        for i in range(8):
            if i & step:
                continue
            a, b = parts[i], parts[i + step]
            parts[i] = jnp.where(low, a, pltpu.roll(b, step * LON_DEV, 1))
            parts[i + step] = jnp.where(low, pltpu.roll(a, LANES - step * LON_DEV, 1), b)
    return parts


def pack_kernel(per_step, x_ref, o_ref):
    def pair(b, carry):
        rows = []
        for e in range(2):
            cells = x_ref[:, b * 2 + e].astype(jnp.float32)
            rows.append(jnp.transpose(cells, (1, 0, 2)))
        halves = []
        for p in range(2):
            halves.append(
                swap_groups([rows[e][p * 4 + r] for e in range(2) for r in range(4)], 1)
            )
        for a in range(8):
            both = jnp.concatenate([halves[0][a], halves[1][a]], axis=0)
            o_ref[a, b] = both.astype(jnp.bfloat16)
        return carry

    lax.fori_loop(0, per_step, pair, 0)


def pack(background, first, count, per_step):
    base = first // per_step
    return pl.pallas_call(
        functools.partial(pack_kernel, per_step),
        out_shape=jax.ShapeDtypeStruct((32, count, 16, LANES), jnp.bfloat16),
        grid=(count // per_step, 4),
        in_specs=[
            pl.BlockSpec((MEM_DEV, 2 * per_step, 8, LANES), lambda i, g: (0, base + i, 0, g))
        ],
        out_specs=pl.BlockSpec((8, per_step, 16, LANES), lambda i, g: (g, i, 0, 0)),
        cost_estimate=pl.CostEstimate(
            flops=count * 65536 * 40, bytes_accessed=count * 262144, transcendentals=0
        ),
        name="pack",
    )(background)


def unpack_kernel(per_step, x_ref, *rest):
    o_ref = rest[-1]

    def pair(b, carry):
        both = [x_ref[a, b].astype(jnp.float32) for a in range(8)]
        rows = [[None] * 8, [None] * 8]
        for p in range(2):
            parts = swap_groups([both[a][p * 8 : (p + 1) * 8] for a in range(8)], -1)
            for e in range(2):
                for r in range(4):
                    rows[e][p * 4 + r] = parts[e * 4 + r]
        for e in range(2):
            cells = jnp.transpose(jnp.stack(rows[e], axis=0), (1, 0, 2))
            o_ref[:, b * 2 + e] = cells.astype(jnp.bfloat16)
        return carry

    lax.fori_loop(0, per_step, pair, 0)


def unpack(blocks, previous, first, count, per_step, shape):
    base = first // per_step
    in_specs = [pl.BlockSpec((8, per_step, 16, LANES), lambda i, g: (g, i, 0, 0))]
    operands = [blocks]
    aliases = {}
    if previous is not None:
        in_specs.append(pl.BlockSpec(memory_space=pl.ANY))
        operands.append(previous)
        aliases = {1: 0}
    return pl.pallas_call(
        functools.partial(unpack_kernel, per_step),
        out_shape=jax.ShapeDtypeStruct(shape, jnp.bfloat16),
        grid=(count // per_step, 4),
        in_specs=in_specs,
        out_specs=pl.BlockSpec(
            (MEM_DEV, 2 * per_step, 8, LANES), lambda i, g: (0, base + i, 0, g)
        ),
        input_output_aliases=aliases,
        cost_estimate=pl.CostEstimate(
            flops=count * 65536 * 40, bytes_accessed=count * 262144, transcendentals=0
        ),
        name="unpack",
    )(*operands)


def gather_kernel(counts, tiles, info_ref, *refs):
    blocks, o_ref, held = refs[: len(counts)], refs[-2], refs[-1]
    step = pl.program_id(0)
    lane_index = lax.broadcasted_iota(jnp.int32, (LANES, 256), 0)
    for t in range(tiles):
        a = step * tiles + t
        info = info_ref[a]
        cell = info[0:1].astype(jnp.int32)
        channel = info[1:2].astype(jnp.int32)
        lane = (channel & 1) * 64 + (cell & 63)
        group = (channel >> 1) * 2 + (cell >> 6)
        pick = (lane_index == lane).astype(jnp.float32).astype(jnp.bfloat16)
        total = jnp.zeros((MEM_DEV, 256), jnp.float32)
        first = 0
        for block, count in zip(blocks, counts):
            rows = block[t].reshape(count * 16, LANES)
            found = lax.dot_general(rows, pick, NN, preferred_element_type=jnp.float32)
            found = found.reshape(count * 2, MEM_DEV, 256)
            for g in range(count * 2):
                total = total + jnp.where(group == first * 2 + g, found[g], 0.0)
            first += count
        held[lax.rem(a + 1, 32), 0:8] = total
        held[a, 8:16] = total
        held[lax.rem(a + 31, 32), 16:24] = total

    @pl.when(step == 32 // tiles - 1)
    def _():
        o_ref[...] = held[...].astype(jnp.bfloat16)


def gather_obs(info, blocks):
    counts = tuple(b.shape[1] for b in blocks)
    tiles = 4
    return pl.pallas_call(
        functools.partial(gather_kernel, counts, tiles),
        out_shape=jax.ShapeDtypeStruct((32, 24, 256), jnp.bfloat16),
        grid=(32 // tiles,),
        in_specs=[pl.BlockSpec((32, 4, 256), lambda i: (0, 0, 0))]
        + [pl.BlockSpec((tiles, c, 16, LANES), lambda i: (i, 0, 0, 0)) for c in counts],
        out_specs=pl.BlockSpec((32, 24, 256), lambda i: (0, 0, 0)),
        scratch_shapes=[pltpu.VMEM((32, 24, 256), jnp.float32)],
        compiler_params=pltpu.CompilerParams(vmem_limit_bytes=VMEM_LIMIT),
        cost_estimate=pl.CostEstimate(
            flops=2 * 32 * 640 * 256 * 128, bytes_accessed=6 << 20, transcendentals=0
        ),
        name="gather_obs",
    )(info, *blocks)


def split(x):
    high = x.astype(jnp.bfloat16)
    return high, (x - high.astype(jnp.float32)).astype(jnp.bfloat16)


def product(a, b, dims):
    a_high, a_low = a if isinstance(a, tuple) else split(a)
    b_high, b_low = b if isinstance(b, tuple) else split(b)
    dot = functools.partial(
        lax.dot_general, dimension_numbers=dims, preferred_element_type=jnp.float32
    )
    return dot(a_high, b_high) + (dot(a_high, b_low) + dot(a_low, b_high))


def weights_kernel(own, below, above, own_info, below_info, above_info, w_ref, keep_ref, gram):
    members = 256
    row_id = lax.broadcasted_iota(jnp.int32, (members, members), 0)
    col_id = lax.broadcasted_iota(jnp.int32, (members, members), 1)
    identity = (row_id == col_id).astype(jnp.float32)
    drive = [jnp.zeros((8, members), jnp.float32) for _ in range(2)]
    first = True
    lon_centre = (LON_DEV - 1) / 2.0
    for j, (values, infos) in enumerate(
        ((below, below_info), (own, own_info), (above, above_info))
    ):
        lat_shift = (j - 1.0) * LAT_DEV
        for i in range(3):
            lon_shift = (i - 1.0) * LON_DEV
            hx = values[...].astype(jnp.float32).reshape(32, 3, MEM_DEV, 256)[:, i]
            hx = hx.reshape(members, 256)
            centre = jnp.sum(hx, axis=0, keepdims=True) * (1.0 / members)
            y = hx - centre
            y_parts = split(y)
            info = infos[i]
            cell = info[0:1].astype(jnp.int32)
            departure = info[2:3] - centre
            weight = info[3:4]
            lat = (cell >> 4).astype(jnp.float32) + lat_shift
            lon = (cell & 15).astype(jnp.float32) + lon_shift
            for p in range(2):
                lat_centre = p * PATCH_LAT + (PATCH_LAT - 1) / 2.0
                dist = (lat - lat_centre) ** 2 + (lon - lon_centre) ** 2
                obs_weight = jnp.exp(-dist / (2.0 * LOC * LOC)) * weight
                term = product(y * obs_weight, y_parts, NT)
                if first:
                    gram[p] = identity + term
                else:
                    gram[p] += term
                pull = jnp.broadcast_to(obs_weight * departure, (8, 256))
                drive[p] = drive[p] + product(pull, y_parts, NT)
            first = False
    roots, inverses, scales = [], [], []
    for p in range(2):
        system = gram[p]
        scale = jnp.sqrt(jnp.sum(jnp.sum(system * system, axis=0, keepdims=True), axis=1, keepdims=True))
        roots.append(system / scale)
        scales.append(scale)
    for step in range(NS_ITERS):
        for p in range(2):
            if step == 0:
                factor = 1.5 * identity - 0.5 * roots[p]
                f_parts = split(factor)
                roots[p] = product(roots[p], f_parts, NN)
                inverses_p = factor
                if len(inverses) < 2:
                    inverses.append(inverses_p)
            else:
                i_parts = split(inverses[p])
                r_parts = split(roots[p])
                factor = 1.5 * identity - 0.5 * product(i_parts, r_parts, NN)
                f_parts = split(factor)
                if step < NS_ITERS - 1:
                    roots[p] = product(r_parts, f_parts, NN)
                inverses[p] = product(f_parts, i_parts, NN)
    for p in range(2):
        spread = inverses[p] / jnp.sqrt(scales[p])
        s_parts = split(spread)
        shift = product(product(drive[p], s_parts, NT), s_parts, NT)
        weights = (spread + shift[0:1]).astype(jnp.bfloat16)
        w_ref[p] = weights
        total = jnp.sum(weights.astype(jnp.float32), axis=1, keepdims=True)
        keep_ref[p] = jnp.broadcast_to(1.0 - total, (members, LANES))


def tile_weights(values, infos):
    vmem = pl.BlockSpec(memory_space=pltpu.VMEM)
    return pl.pallas_call(
        weights_kernel,
        out_shape=(
            jax.ShapeDtypeStruct((2, 256, 256), jnp.bfloat16),
            jax.ShapeDtypeStruct((2, 256, LANES), jnp.float32),
        ),
        in_specs=[vmem] * 6,
        out_specs=(vmem, vmem),
        scratch_shapes=[pltpu.VMEM((2, 256, 256), jnp.float32)],
        compiler_params=pltpu.CompilerParams(vmem_limit_bytes=VMEM_LIMIT),
        cost_estimate=pl.CostEstimate(
            flops=2 * 160 * 256**3, bytes_accessed=3 << 20, transcendentals=0
        ),
        name="tile_weights",
    )(*values, *infos)


def transform_kernel(per_step, x_ref, w_ref, keep_ref, o_ref):
    for b in range(per_step):
        both = x_ref[:, b].astype(jnp.float32).reshape(32, 2, MEM_DEV, LANES)
        outs = []
        for p in range(2):
            states = both[:, p].reshape(256, LANES)
            mean = jnp.sum(states, axis=0, keepdims=True) * (1.0 / 256.0)
            mixed = lax.dot_general(
                w_ref[p], states.astype(jnp.bfloat16), NN, preferred_element_type=jnp.float32
            )
            result = mixed + keep_ref[p] * mean
            outs.append(result.reshape(32, 1, MEM_DEV, LANES))
        result = jnp.concatenate(outs, axis=1).reshape(32, 16, LANES)
        o_ref[:, b] = result.astype(jnp.bfloat16)


def transform(blocks, weights, keep, per_step):
    count = blocks.shape[1]
    spec = pl.BlockSpec((32, per_step, 16, LANES), lambda i: (0, i, 0, 0))
    return pl.pallas_call(
        functools.partial(transform_kernel, per_step),
        out_shape=jax.ShapeDtypeStruct(blocks.shape, jnp.bfloat16),
        grid=(count // per_step,),
        in_specs=[
            spec,
            pl.BlockSpec((2, 256, 256), lambda i: (0, 0, 0)),
            pl.BlockSpec((2, 256, LANES), lambda i: (0, 0, 0)),
        ],
        out_specs=spec,
        compiler_params=pltpu.CompilerParams(vmem_limit_bytes=VMEM_LIMIT),
        cost_estimate=pl.CostEstimate(
            flops=count * 4 * 256 * 256 * 128, bytes_accessed=count * 262144, transcendentals=0
        ),
        name="transform",
    )(blocks, weights, keep)


def exchange(blocks):
    return lax.all_to_all(blocks, "member", split_axis=0, concat_axis=0, tiled=True)


def per_device(background, obs_cell, obs_channel, obs_count, obs_value, obs_precision):
    firsts = [sum(CHUNKS[:n]) for n in range(len(CHUNKS))]
    slots = obs_cell.shape[-1]
    members = 256
    blocks = [pack(background, f, c, 5) for f, c in zip(firsts, CHUNKS)]
    arrived = [exchange(b) for b in blocks]

    inside = (jnp.arange(slots, dtype=jnp.int32) < obs_count[0, 0]).astype(jnp.float32)
    weight = inside * obs_precision[0, 0] / (members - 1.0)
    own = jnp.stack(
        [
            obs_cell[0, 0].astype(jnp.float32),
            obs_channel[0, 0].astype(jnp.float32),
            obs_value[0, 0],
            weight,
        ]
    )
    info = lax.all_gather(own, "member")
    hx = exchange(gather_obs(info, blocks))
    me = lax.axis_index("member")
    near = jnp.stack(
        [
            lax.dynamic_index_in_dim(info, lax.rem(me + d, 32), 0, keepdims=False)
            for d in (31, 0, 1)
        ]
    )
    bands = lax.axis_size("tile")
    up = [(i, i + 1) for i in range(bands - 1)]
    down = [(i + 1, i) for i in range(bands - 1)]
    values = (hx, lax.ppermute(hx, "tile", up), lax.ppermute(hx, "tile", down))
    infos = (near, lax.ppermute(near, "tile", up), lax.ppermute(near, "tile", down))
    weights, keep = tile_weights(values, infos)

    back = [exchange(transform(b, weights, keep, 2)) for b in arrived]
    out = None
    for b, f, c in zip(back, firsts, CHUNKS):
        out = unpack(b, out, f, c, 5, background.shape)
    return out


def solution(mesh):
    in_specs = (
        P("member", None, "tile", None),
        P("member", "tile", None),
        P("member", "tile", None),
        P("member", "tile"),
        P("member", "tile", None),
        P("member", "tile", None),
    )
    out_specs = P("member", None, "tile", None)
    return jax.shard_map(
        per_device, mesh=mesh, in_specs=in_specs, out_specs=out_specs, check_vma=False
    )
```

```python
import functools

import jax
import jax.numpy as jnp
from jax import lax
from jax.experimental import pallas as pl
from jax.experimental.pallas import tpu as pltpu
from jax.sharding import PartitionSpec as P

LAT_DEV = 8
LON_DEV = 16
PATCH_LAT = 4
NS_ITERS = 6
LOC = 8
MEM_DEV = 8
LANES = 128
CHUNKS = (16, 12, 12)
CARRIER = 1
PER_STEP = 4
NT = (((1,), (1,)), ((), ()))
NN = (((1,), (0,)), ((), ()))
VMEM_LIMIT = 48 * 1024 * 1024


def swap_groups(parts):
    lane_group = lax.broadcasted_iota(jnp.int32, parts[0].shape, 1) // LON_DEV
    parts = list(parts)
    for step in (4, 2, 1):
        low = (lane_group & step) == 0
        for i in range(8):
            if i & step:
                continue
            a, b = parts[i], parts[i + step]
            if step == 4:
                crossed = pltpu.roll(jnp.where(low, b, a), 64, 1)
                parts[i] = jnp.where(low, a, crossed)
                parts[i + step] = jnp.where(low, crossed, b)
            else:
                parts[i] = jnp.where(low, a, pltpu.roll(b, step * LON_DEV, 1))
                parts[i + step] = jnp.where(low, pltpu.roll(a, LANES - step * LON_DEV, 1), b)
    return parts


def lanes_of(g):
    return pl.ds(pl.multiple_of(g * LANES, LANES), LANES)


def pack_kernel(per_step, x_ref, o_ref, held):
    def unit(t, carry):
        b, g = t // 4, t % 4
        for e in range(2):
            cells = x_ref[:, b * 2 + e, :, lanes_of(g)].astype(jnp.float32)
            held[t * 2 + e] = cells.reshape(64, LANES)
        parts = []
        for e in range(2):
            for r in range(PATCH_LAT):
                halves = [
                    held[t * 2 + e, pl.ds(p * PATCH_LAT + r, MEM_DEV, stride=8), :]
                    for p in range(2)
                ]
                parts.append(jnp.concatenate(halves, axis=0).astype(jnp.bfloat16))
        for a, part in enumerate(swap_groups(parts)):
            o_ref[g * 8 + a, b] = part
        return carry

    lax.fori_loop(0, per_step * 4, unit, 0, unroll=8)


def relayout_cost(count):
    return pl.CostEstimate(
        flops=count * 65536 * 40, bytes_accessed=count * 262144, transcendentals=0
    )


def pack(background, first, count, extra):
    base = first // PER_STEP
    return pl.pallas_call(
        functools.partial(pack_kernel, PER_STEP),
        out_shape=jax.ShapeDtypeStruct((32, count + extra, 16, LANES), jnp.bfloat16),
        grid=(count // PER_STEP,),
        in_specs=[
            pl.BlockSpec((MEM_DEV, 2 * PER_STEP, 8, 512), lambda i: (0, base + i, 0, 0))
        ],
        out_specs=pl.BlockSpec((32, PER_STEP, 16, LANES), lambda i: (0, i, 0, 0)),
        scratch_shapes=[pltpu.VMEM((8 * PER_STEP, 64, LANES), jnp.float32)],
        compiler_params=pltpu.CompilerParams(vmem_limit_bytes=VMEM_LIMIT),
        cost_estimate=relayout_cost(count),
        name="pack",
    )(background)


def unpack_kernel(per_step, x_ref, *rest):
    o_ref, held = rest[-2:]

    def unit(t, carry):
        b, g = t // 4, t % 4
        parts = swap_groups([x_ref[g * 8 + a, b] for a in range(8)])
        for e in range(2):
            for r in range(PATCH_LAT):
                both = parts[e * PATCH_LAT + r].astype(jnp.float32)
                for p in range(2):
                    held[t * 2 + e, pl.ds(p * PATCH_LAT + r, MEM_DEV, stride=8), :] = both[
                        p * 8 : (p + 1) * 8
                    ]
        for e in range(2):
            cells = held[t * 2 + e].reshape(MEM_DEV, 8, LANES)
            o_ref[:, b * 2 + e, :, lanes_of(g)] = cells.astype(jnp.bfloat16)
        return carry

    lax.fori_loop(0, per_step * 4, unit, 0, unroll=8)


def unpack(blocks, previous, first, count, shape):
    base = first // PER_STEP
    in_specs = [pl.BlockSpec((32, PER_STEP, 16, LANES), lambda i: (0, i, 0, 0))]
    operands = [blocks]
    aliases = {}
    if previous is not None:
        in_specs.append(pl.BlockSpec(memory_space=pl.ANY))
        operands.append(previous)
        aliases = {1: 0}
    return pl.pallas_call(
        functools.partial(unpack_kernel, PER_STEP),
        out_shape=jax.ShapeDtypeStruct(shape, jnp.bfloat16),
        grid=(count // PER_STEP,),
        in_specs=in_specs,
        out_specs=pl.BlockSpec(
            (MEM_DEV, 2 * PER_STEP, 8, 512), lambda i: (0, base + i, 0, 0)
        ),
        scratch_shapes=[pltpu.VMEM((8 * PER_STEP, 64, LANES), jnp.float32)],
        input_output_aliases=aliases,
        compiler_params=pltpu.CompilerParams(vmem_limit_bytes=VMEM_LIMIT),
        cost_estimate=relayout_cost(count),
        name="unpack",
    )(*operands)


def gather_kernel(counts, tiles, info_ref, *refs):
    blocks, o_ref, held = refs[: len(counts)], refs[-2], refs[-1]
    step = pl.program_id(0)
    lane_index = lax.broadcasted_iota(jnp.int32, (LANES, 256), 0)
    for t in range(tiles):
        a = step * tiles + t
        info = info_ref[a]
        cell = info[0:1].astype(jnp.int32)
        channel = info[1:2].astype(jnp.int32)
        lane = (channel & 1) * 64 + (cell & 63)
        group = (channel >> 1) * 2 + (cell >> 6)
        pick = (lane_index == lane).astype(jnp.float32).astype(jnp.bfloat16)
        total = jnp.zeros((MEM_DEV, 256), jnp.float32)
        first = 0
        for block, count in zip(blocks, counts):
            rows = block[t, :count].reshape(count * 16, LANES)
            found = lax.dot_general(rows, pick, NN, preferred_element_type=jnp.float32)
            found = found.reshape(count * 2, MEM_DEV, 256)
            for g in range(count * 2):
                total = total + jnp.where(group == first * 2 + g, found[g], 0.0)
            first += count
        for half in range(2):
            part = total[:, half * LANES : (half + 1) * LANES]
            rows = pl.ds(half * 8, 8)
            held[lax.rem(a + 1, 32), 0, rows] = part
            held[a, 1, rows] = part
            held[lax.rem(a + 31, 32), 2, rows] = part

    @pl.when(step == 32 // tiles - 1)
    def _():
        o_ref[...] = held[...].astype(jnp.bfloat16)


def gather_obs(info, blocks):
    tiles = 4
    carrier = blocks[CARRIER]
    place = CHUNKS[CARRIER] // 3
    return pl.pallas_call(
        functools.partial(gather_kernel, CHUNKS, tiles),
        out_shape=jax.ShapeDtypeStruct(carrier.shape, jnp.bfloat16),
        grid=(32 // tiles,),
        in_specs=[pl.BlockSpec((32, 4, 256), lambda i: (0, 0, 0))]
        + [pl.BlockSpec((tiles,) + b.shape[1:], lambda i: (i, 0, 0, 0)) for b in blocks],
        out_specs=pl.BlockSpec((32, 3, 16, LANES), lambda i: (0, place, 0, 0)),
        scratch_shapes=[pltpu.VMEM((32, 3, 16, LANES), jnp.float32)],
        input_output_aliases={1 + CARRIER: 0},
        compiler_params=pltpu.CompilerParams(vmem_limit_bytes=VMEM_LIMIT),
        cost_estimate=pl.CostEstimate(
            flops=2 * 32 * 640 * 256 * 128, bytes_accessed=6 << 20, transcendentals=0
        ),
        name="gather_obs",
    )(info, *blocks)


def split(x):
    high = x.astype(jnp.bfloat16)
    return high, (x - high.astype(jnp.float32)).astype(jnp.bfloat16)


def product(a, b, dims):
    a_high, a_low = a if isinstance(a, tuple) else split(a)
    b_high, b_low = b if isinstance(b, tuple) else split(b)
    dot = functools.partial(
        lax.dot_general, dimension_numbers=dims, preferred_element_type=jnp.float32
    )
    return dot(a_high, b_high) + (dot(a_high, b_low) + dot(a_low, b_high))


def weights_kernel(own, below, above, own_info, below_info, above_info, w_ref, keep_ref, gram):
    members = 256
    row_id = lax.broadcasted_iota(jnp.int32, (members, members), 0)
    col_id = lax.broadcasted_iota(jnp.int32, (members, members), 1)
    identity = (row_id == col_id).astype(jnp.float32)
    drive = [jnp.zeros((8, members), jnp.float32) for _ in range(2)]
    first = True
    lon_centre = (LON_DEV - 1) / 2.0
    for j, (values, infos) in enumerate(
        ((below, below_info), (own, own_info), (above, above_info))
    ):
        lat_shift = (j - 1.0) * LAT_DEV
        for i in range(3):
            lon_shift = (i - 1.0) * LON_DEV
            halves = values[:, i].astype(jnp.float32).reshape(32, 2, MEM_DEV, LANES)
            hx = jnp.concatenate(
                [halves[:, half].reshape(members, LANES) for half in range(2)], axis=1
            )
            centre = jnp.sum(hx, axis=0, keepdims=True) * (1.0 / members)
            y = hx - centre
            y_parts = split(y)
            info = infos[i]
            cell = info[0:1].astype(jnp.int32)
            departure = info[2:3] - centre
            weight = info[3:4]
            lat = (cell >> 4).astype(jnp.float32) + lat_shift
            lon = (cell & 15).astype(jnp.float32) + lon_shift
            for p in range(2):
                lat_centre = p * PATCH_LAT + (PATCH_LAT - 1) / 2.0
                dist = (lat - lat_centre) ** 2 + (lon - lon_centre) ** 2
                obs_weight = jnp.exp(-dist / (2.0 * LOC * LOC)) * weight
                term = product(y * obs_weight, y_parts, NT)
                if first:
                    gram[p] = identity + term
                else:
                    gram[p] += term
                pull = jnp.broadcast_to(obs_weight * departure, (8, 256))
                drive[p] = drive[p] + product(pull, y_parts, NT)
            first = False
    roots, inverses, scales = [], [], []
    for p in range(2):
        system = gram[p]
        scale = jnp.sqrt(jnp.sum(jnp.sum(system * system, axis=0, keepdims=True), axis=1, keepdims=True))
        roots.append(system / scale)
        scales.append(scale)
    for step in range(NS_ITERS):
        for p in range(2):
            if step == 0:
                factor = 1.5 * identity - 0.5 * roots[p]
                f_parts = split(factor)
                roots[p] = product(roots[p], f_parts, NN)
                inverses_p = factor
                if len(inverses) < 2:
                    inverses.append(inverses_p)
            else:
                i_parts = split(inverses[p])
                r_parts = split(roots[p])
                factor = 1.5 * identity - 0.5 * product(i_parts, r_parts, NN)
                f_parts = split(factor)
                if step < NS_ITERS - 1:
                    roots[p] = product(r_parts, f_parts, NN)
                inverses[p] = product(f_parts, i_parts, NN)
    for p in range(2):
        spread = inverses[p] / jnp.sqrt(scales[p])
        s_parts = split(spread)
        shift = product(product(drive[p], s_parts, NT), s_parts, NT)
        weights = (spread + shift[0:1]).astype(jnp.bfloat16)
        w_ref[p] = weights
        total = jnp.sum(weights.astype(jnp.float32), axis=1, keepdims=True)
        keep_ref[p] = jnp.broadcast_to(1.0 - total, (members, LANES))


def tile_weights(values, infos):
    place = CHUNKS[CARRIER] // 3
    return pl.pallas_call(
        weights_kernel,
        out_shape=(
            jax.ShapeDtypeStruct((2, 256, 256), jnp.bfloat16),
            jax.ShapeDtypeStruct((2, 256, LANES), jnp.float32),
        ),
        grid=(1,),
        in_specs=[
            pl.BlockSpec((32, 3, 16, LANES), lambda i: (0, place, 0, 0)),
            pl.BlockSpec((32, 3, 16, LANES), lambda i: (0, 0, 0, 0)),
            pl.BlockSpec((32, 3, 16, LANES), lambda i: (0, 0, 0, 0)),
        ]
        + [pl.BlockSpec((3, 4, 256), lambda i: (0, 0, 0))] * 3,
        out_specs=(
            pl.BlockSpec((2, 256, 256), lambda i: (0, 0, 0)),
            pl.BlockSpec((2, 256, LANES), lambda i: (0, 0, 0)),
        ),
        scratch_shapes=[pltpu.VMEM((2, 256, 256), jnp.float32)],
        compiler_params=pltpu.CompilerParams(vmem_limit_bytes=VMEM_LIMIT),
        cost_estimate=pl.CostEstimate(
            flops=2 * 160 * 256**3, bytes_accessed=3 << 20, transcendentals=0
        ),
        name="tile_weights",
    )(*values, *infos)


def transform_kernel(per_step, x_ref, w_ref, keep_ref, o_ref):
    for b in range(per_step):
        both = x_ref[:, b].astype(jnp.float32).reshape(32, 2, MEM_DEV, LANES)
        outs = []
        for p in range(2):
            states = both[:, p].reshape(256, LANES)
            mean = jnp.sum(states, axis=0, keepdims=True) * (1.0 / 256.0)
            mixed = lax.dot_general(
                w_ref[p], states.astype(jnp.bfloat16), NN, preferred_element_type=jnp.float32
            )
            result = mixed + keep_ref[p] * mean
            outs.append(result.reshape(32, 1, MEM_DEV, LANES))
        result = jnp.concatenate(outs, axis=1).reshape(32, 16, LANES)
        o_ref[:, b] = result.astype(jnp.bfloat16)


def transform(blocks, count, weights, keep, per_step):
    spec = pl.BlockSpec((32, per_step, 16, LANES), lambda i: (0, i, 0, 0))
    return pl.pallas_call(
        functools.partial(transform_kernel, per_step),
        out_shape=jax.ShapeDtypeStruct((32, count, 16, LANES), jnp.bfloat16),
        grid=(count // per_step,),
        in_specs=[
            spec,
            pl.BlockSpec((2, 256, 256), lambda i: (0, 0, 0)),
            pl.BlockSpec((2, 256, LANES), lambda i: (0, 0, 0)),
        ],
        out_specs=spec,
        compiler_params=pltpu.CompilerParams(vmem_limit_bytes=VMEM_LIMIT),
        cost_estimate=pl.CostEstimate(
            flops=count * 4 * 256 * 256 * 128, bytes_accessed=count * 262144, transcendentals=0
        ),
        name="transform",
    )(blocks, weights, keep)


def exchange(blocks):
    return lax.all_to_all(blocks, "member", split_axis=0, concat_axis=0, tiled=True)


def per_device(background, obs_cell, obs_channel, obs_count, obs_value, obs_precision):
    firsts = [sum(CHUNKS[:n]) for n in range(len(CHUNKS))]
    slots = obs_cell.shape[-1]
    members = 256
    blocks = [
        pack(background, f, c, 3 if n == CARRIER else 0)
        for n, (f, c) in enumerate(zip(firsts, CHUNKS))
    ]

    inside = (jnp.arange(slots, dtype=jnp.int32) < obs_count[0, 0]).astype(jnp.float32)
    weight = inside * obs_precision[0, 0] / (members - 1.0)
    own = jnp.stack(
        [
            obs_cell[0, 0].astype(jnp.float32),
            obs_channel[0, 0].astype(jnp.float32),
            obs_value[0, 0],
            weight,
        ]
    )
    info = exchange(jnp.broadcast_to(own[None], (32,) + own.shape))
    blocks[CARRIER] = gather_obs(info, blocks)
    arrived = [exchange(b) for b in blocks]
    hx = arrived[CARRIER][:, CHUNKS[CARRIER] :]
    me = lax.axis_index("member")
    near = jnp.stack(
        [
            lax.dynamic_index_in_dim(info, lax.rem(me + d, 32), 0, keepdims=False)
            for d in (31, 0, 1)
        ]
    )
    bands = lax.axis_size("tile")
    up = [(i, i + 1) for i in range(bands - 1)]
    down = [(i + 1, i) for i in range(bands - 1)]
    values = (arrived[CARRIER], lax.ppermute(hx, "tile", up), lax.ppermute(hx, "tile", down))
    infos = (near, lax.ppermute(near, "tile", up), lax.ppermute(near, "tile", down))
    weights, keep = tile_weights(values, infos)

    back = [
        exchange(transform(b, c, weights, keep, 4)) for b, c in zip(arrived, CHUNKS)
    ]
    out = None
    for b, f, c in zip(back, firsts, CHUNKS):
        out = unpack(b, out, f, c, background.shape)
    return out


def solution(mesh):
    in_specs = (
        P("member", None, "tile", None),
        P("member", "tile", None),
        P("member", "tile", None),
        P("member", "tile"),
        P("member", "tile", None),
        P("member", "tile", None),
    )
    out_specs = P("member", None, "tile", None)
    return jax.shard_map(
        per_device, mesh=mesh, in_specs=in_specs, out_specs=out_specs, check_vma=False
    )
```

```python
import functools

import jax
import jax.numpy as jnp
from jax import lax
from jax.experimental import pallas as pl
from jax.experimental.pallas import tpu as pltpu
from jax.sharding import PartitionSpec as P

LAT_DEV = 8
LON_DEV = 16
PATCH_LAT = 4
NS_ITERS = 6
LOC = 8
MEM_DEV = 8
LANES = 128
CHUNKS = (20, 12, 8)
CARRIER = 1
PER_STEP = 4
NT = (((1,), (1,)), ((), ()))
NN = (((1,), (0,)), ((), ()))
VMEM_LIMIT = 48 * 1024 * 1024


def swap_groups(parts):
    lane_group = lax.broadcasted_iota(jnp.int32, parts[0].shape, 1) // LON_DEV
    parts = list(parts)
    for step in (4, 2, 1):
        low = (lane_group & step) == 0
        for i in range(8):
            if i & step:
                continue
            a, b = parts[i], parts[i + step]
            if step == 4:
                crossed = pltpu.roll(jnp.where(low, b, a), 64, 1)
                parts[i] = jnp.where(low, a, crossed)
                parts[i + step] = jnp.where(low, crossed, b)
            else:
                parts[i] = jnp.where(low, a, pltpu.roll(b, step * LON_DEV, 1))
                parts[i + step] = jnp.where(low, pltpu.roll(a, LANES - step * LON_DEV, 1), b)
    return parts


def lanes_of(g):
    return pl.ds(pl.multiple_of(g * LANES, LANES), LANES)


def pack_block(per_step, held, x_ref, o_ref):
    def unit(t, carry):
        b, g = t // 4, t % 4
        for e in range(2):
            cells = x_ref[:, b * 2 + e, :, lanes_of(g)].astype(jnp.float32)
            held[t * 2 + e] = cells.reshape(64, LANES)
        parts = []
        for e in range(2):
            for r in range(PATCH_LAT):
                halves = [
                    held[t * 2 + e, pl.ds(p * PATCH_LAT + r, MEM_DEV, stride=8), :]
                    for p in range(2)
                ]
                parts.append(jnp.concatenate(halves, axis=0).astype(jnp.bfloat16))
        for a, part in enumerate(swap_groups(parts)):
            o_ref[g * 8 + a, b] = part
        return carry

    lax.fori_loop(0, per_step * 4, unit, 0, unroll=8)


def pack_kernel(turn, ranges, parity_ref, x_ref, *refs):
    outs, held = refs[-1 - len(ranges) : -1], refs[-1]

    @pl.when(parity_ref[0] == turn)
    def _():
        for (first, count), o_ref in zip(ranges, outs):
            base = first // PER_STEP
            pltpu.emit_pipeline(
                functools.partial(pack_block, PER_STEP, held),
                grid=(count // PER_STEP,),
                in_specs=[
                    pl.BlockSpec(
                        (MEM_DEV, 2 * PER_STEP, 8, 512), lambda i, base=base: (0, base + i, 0, 0)
                    )
                ],
                out_specs=[pl.BlockSpec((32, PER_STEP, 16, LANES), lambda i: (0, i, 0, 0))],
            )(x_ref, o_ref)


def pack(turn, parity, background, chunks, previous=(), after=()):
    anywhere = pl.BlockSpec(memory_space=pl.ANY)
    firsts = [sum(CHUNKS[:n]) for n in chunks]
    ranges = tuple((f, CHUNKS[n]) for f, n in zip(firsts, chunks))
    return pl.pallas_call(
        functools.partial(pack_kernel, turn, ranges),
        out_shape=tuple(
            jax.ShapeDtypeStruct(
                (32, CHUNKS[n] + (3 if n == CARRIER else 0), 16, LANES), jnp.bfloat16
            )
            for n in chunks
        ),
        in_specs=[pl.BlockSpec(memory_space=pltpu.SMEM), anywhere]
        + [anywhere] * (len(previous) + len(after)),
        out_specs=(anywhere,) * len(chunks),
        scratch_shapes=[pltpu.VMEM((8 * PER_STEP, 64, LANES), jnp.float32)],
        input_output_aliases={2 + n: n for n in range(len(previous))},
        compiler_params=pltpu.CompilerParams(vmem_limit_bytes=VMEM_LIMIT),
        cost_estimate=relayout_cost(sum(count for _, count in ranges)),
        name="pack",
    )(parity, background, *previous, *after)


def relayout_cost(count):
    return pl.CostEstimate(
        flops=count * 65536 * 40, bytes_accessed=count * 262144, transcendentals=0
    )


def unpack_kernel(per_step, x_ref, *rest):
    o_ref, held = rest[-2:]

    def unit(t, carry):
        b, g = t // 4, t % 4
        parts = swap_groups([x_ref[g * 8 + a, b] for a in range(8)])
        for e in range(2):
            for r in range(PATCH_LAT):
                both = parts[e * PATCH_LAT + r].astype(jnp.float32)
                for p in range(2):
                    held[t * 2 + e, pl.ds(p * PATCH_LAT + r, MEM_DEV, stride=8), :] = both[
                        p * 8 : (p + 1) * 8
                    ]
        for e in range(2):
            cells = held[t * 2 + e].reshape(MEM_DEV, 8, LANES)
            o_ref[:, b * 2 + e, :, lanes_of(g)] = cells.astype(jnp.bfloat16)
        return carry

    lax.fori_loop(0, per_step * 4, unit, 0, unroll=8)


def unpack(blocks, previous, first, count, shape):
    base = first // PER_STEP
    in_specs = [pl.BlockSpec((32, PER_STEP, 16, LANES), lambda i: (0, i, 0, 0))]
    operands = [blocks]
    aliases = {}
    if previous is not None:
        in_specs.append(pl.BlockSpec(memory_space=pl.ANY))
        operands.append(previous)
        aliases = {1: 0}
    return pl.pallas_call(
        functools.partial(unpack_kernel, PER_STEP),
        out_shape=jax.ShapeDtypeStruct(shape, jnp.bfloat16),
        grid=(count // PER_STEP,),
        in_specs=in_specs,
        out_specs=pl.BlockSpec(
            (MEM_DEV, 2 * PER_STEP, 8, 512), lambda i: (0, base + i, 0, 0)
        ),
        scratch_shapes=[pltpu.VMEM((8 * PER_STEP, 64, LANES), jnp.float32)],
        input_output_aliases=aliases,
        compiler_params=pltpu.CompilerParams(vmem_limit_bytes=VMEM_LIMIT),
        cost_estimate=relayout_cost(count),
        name="unpack",
    )(*operands)


def gather_kernel(counts, tiles, info_ref, *refs):
    blocks, o_ref, held = refs[: len(counts)], refs[-2], refs[-1]
    step = pl.program_id(0)
    lane_index = lax.broadcasted_iota(jnp.int32, (LANES, 256), 0)
    for t in range(tiles):
        a = step * tiles + t
        info = info_ref[a]
        cell = info[0:1].astype(jnp.int32)
        channel = info[1:2].astype(jnp.int32)
        lane = (channel & 1) * 64 + (cell & 63)
        group = (channel >> 1) * 2 + (cell >> 6)
        pick = (lane_index == lane).astype(jnp.float32).astype(jnp.bfloat16)
        total = jnp.zeros((MEM_DEV, 256), jnp.float32)
        first = 0
        for block, count in zip(blocks, counts):
            rows = block[t, :count].reshape(count * 16, LANES)
            found = lax.dot_general(rows, pick, NN, preferred_element_type=jnp.float32)
            found = found.reshape(count * 2, MEM_DEV, 256)
            for g in range(count * 2):
                total = total + jnp.where(group == first * 2 + g, found[g], 0.0)
            first += count
        for half in range(2):
            part = total[:, half * LANES : (half + 1) * LANES]
            rows = pl.ds(half * 8, 8)
            held[lax.rem(a + 1, 32), 0, rows] = part
            held[a, 1, rows] = part
            held[lax.rem(a + 31, 32), 2, rows] = part

    @pl.when(step == 32 // tiles - 1)
    def _():
        o_ref[...] = held[...].astype(jnp.bfloat16)


def gather_obs(info, blocks):
    tiles = 4
    carrier = blocks[CARRIER]
    place = CHUNKS[CARRIER] // 3
    return pl.pallas_call(
        functools.partial(gather_kernel, CHUNKS, tiles),
        out_shape=jax.ShapeDtypeStruct(carrier.shape, jnp.bfloat16),
        grid=(32 // tiles,),
        in_specs=[pl.BlockSpec((32, 4, 256), lambda i: (0, 0, 0))]
        + [pl.BlockSpec((tiles,) + b.shape[1:], lambda i: (i, 0, 0, 0)) for b in blocks],
        out_specs=pl.BlockSpec((32, 3, 16, LANES), lambda i: (0, place, 0, 0)),
        scratch_shapes=[pltpu.VMEM((32, 3, 16, LANES), jnp.float32)],
        input_output_aliases={1 + CARRIER: 0},
        compiler_params=pltpu.CompilerParams(vmem_limit_bytes=VMEM_LIMIT),
        cost_estimate=pl.CostEstimate(
            flops=2 * 32 * 640 * 256 * 128, bytes_accessed=6 << 20, transcendentals=0
        ),
        name="gather_obs",
    )(info, *blocks)


def split(x):
    high = x.astype(jnp.bfloat16)
    return high, (x - high.astype(jnp.float32)).astype(jnp.bfloat16)


def product(a, b, dims):
    a_high, a_low = a if isinstance(a, tuple) else split(a)
    b_high, b_low = b if isinstance(b, tuple) else split(b)
    dot = functools.partial(
        lax.dot_general, dimension_numbers=dims, preferred_element_type=jnp.float32
    )
    return dot(a_high, b_high) + (dot(a_high, b_low) + dot(a_low, b_high))


def weights_kernel(own, below, above, own_info, below_info, above_info, w_ref, keep_ref, gram):
    members = 256
    row_id = lax.broadcasted_iota(jnp.int32, (members, members), 0)
    col_id = lax.broadcasted_iota(jnp.int32, (members, members), 1)
    identity = (row_id == col_id).astype(jnp.float32)
    drive = [jnp.zeros((8, members), jnp.float32) for _ in range(2)]
    first = True
    lon_centre = (LON_DEV - 1) / 2.0
    for j, (values, infos) in enumerate(
        ((below, below_info), (own, own_info), (above, above_info))
    ):
        lat_shift = (j - 1.0) * LAT_DEV
        for i in range(3):
            lon_shift = (i - 1.0) * LON_DEV
            halves = values[:, i].astype(jnp.float32).reshape(32, 2, MEM_DEV, LANES)
            hx = jnp.concatenate(
                [halves[:, half].reshape(members, LANES) for half in range(2)], axis=1
            )
            centre = jnp.sum(hx, axis=0, keepdims=True) * (1.0 / members)
            y = hx - centre
            y_parts = split(y)
            info = infos[i]
            cell = info[0:1].astype(jnp.int32)
            departure = info[2:3] - centre
            weight = info[3:4]
            lat = (cell >> 4).astype(jnp.float32) + lat_shift
            lon = (cell & 15).astype(jnp.float32) + lon_shift
            for p in range(2):
                lat_centre = p * PATCH_LAT + (PATCH_LAT - 1) / 2.0
                dist = (lat - lat_centre) ** 2 + (lon - lon_centre) ** 2
                obs_weight = jnp.exp(-dist / (2.0 * LOC * LOC)) * weight
                term = product(y * obs_weight, y_parts, NT)
                if first:
                    gram[p] = identity + term
                else:
                    gram[p] += term
                pull = jnp.broadcast_to(obs_weight * departure, (8, 256))
                drive[p] = drive[p] + product(pull, y_parts, NT)
            first = False
    roots, inverses, scales = [], [], []
    for p in range(2):
        system = gram[p]
        scale = jnp.sqrt(jnp.sum(jnp.sum(system * system, axis=0, keepdims=True), axis=1, keepdims=True))
        roots.append(system / scale)
        scales.append(scale)
    for step in range(NS_ITERS):
        for p in range(2):
            if step == 0:
                factor = 1.5 * identity - 0.5 * roots[p]
                f_parts = split(factor)
                roots[p] = product(roots[p], f_parts, NN)
                inverses_p = factor
                if len(inverses) < 2:
                    inverses.append(inverses_p)
            else:
                i_parts = split(inverses[p])
                r_parts = split(roots[p])
                factor = 1.5 * identity - 0.5 * product(i_parts, r_parts, NN)
                f_parts = split(factor)
                if step < NS_ITERS - 1:
                    roots[p] = product(r_parts, f_parts, NN)
                inverses[p] = product(f_parts, i_parts, NN)
    for p in range(2):
        spread = inverses[p] / jnp.sqrt(scales[p])
        s_parts = split(spread)
        shift = product(product(drive[p], s_parts, NT), s_parts, NT)
        weights = (spread + shift[0:1]).astype(jnp.bfloat16)
        w_ref[p] = weights
        total = jnp.sum(weights.astype(jnp.float32), axis=1, keepdims=True)
        keep_ref[p] = jnp.broadcast_to(1.0 - total, (members, LANES))


def tile_weights(values, infos):
    place = CHUNKS[CARRIER] // 3
    return pl.pallas_call(
        weights_kernel,
        out_shape=(
            jax.ShapeDtypeStruct((2, 256, 256), jnp.bfloat16),
            jax.ShapeDtypeStruct((2, 256, LANES), jnp.float32),
        ),
        grid=(1,),
        in_specs=[
            pl.BlockSpec((32, 3, 16, LANES), lambda i: (0, place, 0, 0)),
            pl.BlockSpec((32, 3, 16, LANES), lambda i: (0, 0, 0, 0)),
            pl.BlockSpec((32, 3, 16, LANES), lambda i: (0, 0, 0, 0)),
        ]
        + [pl.BlockSpec((3, 4, 256), lambda i: (0, 0, 0))] * 3,
        out_specs=(
            pl.BlockSpec((2, 256, 256), lambda i: (0, 0, 0)),
            pl.BlockSpec((2, 256, LANES), lambda i: (0, 0, 0)),
        ),
        scratch_shapes=[pltpu.VMEM((2, 256, 256), jnp.float32)],
        compiler_params=pltpu.CompilerParams(vmem_limit_bytes=VMEM_LIMIT),
        cost_estimate=pl.CostEstimate(
            flops=2 * 160 * 256**3, bytes_accessed=3 << 20, transcendentals=0
        ),
        name="tile_weights",
    )(*values, *infos)


def transform_kernel(per_step, x_ref, w_ref, keep_ref, o_ref):
    for b in range(per_step):
        both = x_ref[:, b].astype(jnp.float32).reshape(32, 2, MEM_DEV, LANES)
        outs = []
        for p in range(2):
            states = both[:, p].reshape(256, LANES)
            mean = jnp.sum(states, axis=0, keepdims=True) * (1.0 / 256.0)
            mixed = lax.dot_general(
                w_ref[p], states.astype(jnp.bfloat16), NN, preferred_element_type=jnp.float32
            )
            result = mixed + keep_ref[p] * mean
            outs.append(result.reshape(32, 1, MEM_DEV, LANES))
        result = jnp.concatenate(outs, axis=1).reshape(32, 16, LANES)
        o_ref[:, b] = result.astype(jnp.bfloat16)


def transform(blocks, count, weights, keep, per_step):
    spec = pl.BlockSpec((32, per_step, 16, LANES), lambda i: (0, i, 0, 0))
    return pl.pallas_call(
        functools.partial(transform_kernel, per_step),
        out_shape=jax.ShapeDtypeStruct((32, count, 16, LANES), jnp.bfloat16),
        grid=(count // per_step,),
        in_specs=[
            spec,
            pl.BlockSpec((2, 256, 256), lambda i: (0, 0, 0)),
            pl.BlockSpec((2, 256, LANES), lambda i: (0, 0, 0)),
        ],
        out_specs=spec,
        compiler_params=pltpu.CompilerParams(vmem_limit_bytes=VMEM_LIMIT),
        cost_estimate=pl.CostEstimate(
            flops=count * 4 * 256 * 256 * 128, bytes_accessed=count * 262144, transcendentals=0
        ),
        name="transform",
    )(blocks, weights, keep)


def exchange(blocks):
    return lax.all_to_all(blocks, "member", split_axis=0, concat_axis=0, tiled=True)


def per_device(background, obs_cell, obs_channel, obs_count, obs_value, obs_precision):
    firsts = [sum(CHUNKS[:n]) for n in range(len(CHUNKS))]
    slots = obs_cell.shape[-1]
    members = 256
    inside = (jnp.arange(slots, dtype=jnp.int32) < obs_count[0, 0]).astype(jnp.float32)
    weight = inside * obs_precision[0, 0] / (members - 1.0)
    own = jnp.stack(
        [
            obs_cell[0, 0].astype(jnp.float32),
            obs_channel[0, 0].astype(jnp.float32),
            obs_value[0, 0],
            weight,
        ]
    )
    info = exchange(jnp.broadcast_to(own[None], (32,) + own.shape))
    parity = (1 - (lax.axis_index("tile") & 1)).astype(jnp.int32).reshape(1)
    (lead,) = pack(0, parity, background, (2,))
    lead, *rest = pack(1, parity, background, (2, 0, 1), (lead,), (info,))
    rest = pack(0, parity, background, (0, 1), tuple(rest), (lead,))
    blocks = [rest[0], rest[1], lead]
    blocks[CARRIER] = gather_obs(info, blocks)
    arrived = [exchange(b) for b in blocks]
    hx = arrived[CARRIER][:, CHUNKS[CARRIER] :]
    me = lax.axis_index("member")
    near = jnp.stack(
        [
            lax.dynamic_index_in_dim(info, lax.rem(me + d, 32), 0, keepdims=False)
            for d in (31, 0, 1)
        ]
    )
    bands = lax.axis_size("tile")
    up = [(i, i + 1) for i in range(bands - 1)]
    down = [(i + 1, i) for i in range(bands - 1)]
    values = (arrived[CARRIER], lax.ppermute(hx, "tile", up), lax.ppermute(hx, "tile", down))
    infos = (near, lax.ppermute(near, "tile", up), lax.ppermute(near, "tile", down))
    weights, keep = tile_weights(values, infos)

    back = [
        exchange(transform(b, c, weights, keep, 4)) for b, c in zip(arrived, CHUNKS)
    ]
    out = None
    for b, f, c in zip(back, firsts, CHUNKS):
        out = unpack(b, out, f, c, background.shape)
    return out


def solution(mesh):
    in_specs = (
        P("member", None, "tile", None),
        P("member", "tile", None),
        P("member", "tile", None),
        P("member", "tile"),
        P("member", "tile", None),
        P("member", "tile", None),
    )
    out_specs = P("member", None, "tile", None)
    mapped = jax.shard_map(
        per_device, mesh=mesh, in_specs=in_specs, out_specs=out_specs, check_vma=False
    )

    def run(*args):
        with jax.sharding.use_abstract_mesh(mesh.abstract_mesh):
            return mapped(*args)

    return run
```

```python
import functools

import jax
import jax.numpy as jnp
from jax import lax
from jax.experimental import pallas as pl
from jax.experimental.pallas import tpu as pltpu
from jax.sharding import PartitionSpec as P

LAT_DEV = 8
LON_DEV = 16
PATCH_LAT = 4
NS_ITERS = 6
LOC = 8
MEM_DEV = 8
LANES = 128
CHUNKS = (20, 12, 8)
CARRIER = 1
PER_STEP = 4
NT = (((1,), (1,)), ((), ()))
NN = (((1,), (0,)), ((), ()))
VMEM_LIMIT = 48 * 1024 * 1024


def swap_groups(parts):
    lane_group = lax.broadcasted_iota(jnp.int32, parts[0].shape, 1) // LON_DEV
    parts = list(parts)
    for step in (4, 2, 1):
        low = (lane_group & step) == 0
        for i in range(8):
            if i & step:
                continue
            a, b = parts[i], parts[i + step]
            if step == 4:
                crossed = pltpu.roll(jnp.where(low, b, a), 64, 1)
                parts[i] = jnp.where(low, a, crossed)
                parts[i + step] = jnp.where(low, crossed, b)
            else:
                parts[i] = jnp.where(low, a, pltpu.roll(b, step * LON_DEV, 1))
                parts[i + step] = jnp.where(low, pltpu.roll(a, LANES - step * LON_DEV, 1), b)
    return parts


def lanes_of(g):
    return pl.ds(pl.multiple_of(g * LANES, LANES), LANES)


def pack_block(per_step, held, x_ref, o_ref):
    def unit(t, carry):
        b, g = t // 4, t % 4
        for e in range(2):
            cells = x_ref[:, b * 2 + e, :, lanes_of(g)].astype(jnp.float32)
            held[t * 2 + e] = cells.reshape(64, LANES)
        parts = []
        for e in range(2):
            for r in range(PATCH_LAT):
                halves = [
                    held[t * 2 + e, pl.ds(p * PATCH_LAT + r, MEM_DEV, stride=8), :]
                    for p in range(2)
                ]
                parts.append(jnp.concatenate(halves, axis=0).astype(jnp.bfloat16))
        for a, part in enumerate(swap_groups(parts)):
            o_ref[g * 8 + a, b] = part
        return carry

    lax.fori_loop(0, per_step * 4, unit, 0, unroll=8)


def pack_kernel(turn, ranges, parity_ref, x_ref, *refs):
    outs, held = refs[-1 - len(ranges) : -1], refs[-1]

    @pl.when(parity_ref[0] == turn)
    def _():
        for (first, count), o_ref in zip(ranges, outs):
            base = first // PER_STEP
            pltpu.emit_pipeline(
                functools.partial(pack_block, PER_STEP, held),
                grid=(count // PER_STEP,),
                in_specs=[
                    pl.BlockSpec(
                        (MEM_DEV, 2 * PER_STEP, 8, 512), lambda i, base=base: (0, base + i, 0, 0)
                    )
                ],
                out_specs=[pl.BlockSpec((32, PER_STEP, 16, LANES), lambda i: (0, i, 0, 0))],
            )(x_ref, o_ref)


def pack(turn, parity, background, chunks, previous=(), after=()):
    anywhere = pl.BlockSpec(memory_space=pl.ANY)
    firsts = [sum(CHUNKS[:n]) for n in chunks]
    ranges = tuple((f, CHUNKS[n]) for f, n in zip(firsts, chunks))
    return pl.pallas_call(
        functools.partial(pack_kernel, turn, ranges),
        out_shape=tuple(
            jax.ShapeDtypeStruct(
                (32, CHUNKS[n] + (3 if n == CARRIER else 0), 16, LANES), jnp.bfloat16
            )
            for n in chunks
        ),
        in_specs=[pl.BlockSpec(memory_space=pltpu.SMEM), anywhere]
        + [anywhere] * (len(previous) + len(after)),
        out_specs=(anywhere,) * len(chunks),
        scratch_shapes=[pltpu.VMEM((8 * PER_STEP, 64, LANES), jnp.float32)],
        input_output_aliases={2 + n: n for n in range(len(previous))},
        compiler_params=pltpu.CompilerParams(vmem_limit_bytes=VMEM_LIMIT),
        cost_estimate=relayout_cost(sum(count for _, count in ranges)),
        name="pack",
    )(parity, background, *previous, *after)


def relayout_cost(count):
    return pl.CostEstimate(
        flops=count * 65536 * 40, bytes_accessed=count * 262144, transcendentals=0
    )


def unpack_kernel(per_step, x_ref, *rest):
    o_ref, held = rest[-2:]

    def unit(t, carry):
        b, g = t // 4, t % 4
        parts = swap_groups([x_ref[g * 8 + a, b] for a in range(8)])
        for e in range(2):
            for r in range(PATCH_LAT):
                both = parts[e * PATCH_LAT + r].astype(jnp.float32)
                for p in range(2):
                    held[t * 2 + e, pl.ds(p * PATCH_LAT + r, MEM_DEV, stride=8), :] = both[
                        p * 8 : (p + 1) * 8
                    ]
        for e in range(2):
            cells = held[t * 2 + e].reshape(MEM_DEV, 8, LANES)
            o_ref[:, b * 2 + e, :, lanes_of(g)] = cells.astype(jnp.bfloat16)
        return carry

    lax.fori_loop(0, per_step * 4, unit, 0, unroll=8)


def unpack(blocks, previous, first, count, shape):
    base = first // PER_STEP
    in_specs = [pl.BlockSpec((32, PER_STEP, 16, LANES), lambda i: (0, i, 0, 0))]
    operands = [blocks]
    aliases = {}
    if previous is not None:
        in_specs.append(pl.BlockSpec(memory_space=pl.ANY))
        operands.append(previous)
        aliases = {1: 0}
    return pl.pallas_call(
        functools.partial(unpack_kernel, PER_STEP),
        out_shape=jax.ShapeDtypeStruct(shape, jnp.bfloat16),
        grid=(count // PER_STEP,),
        in_specs=in_specs,
        out_specs=pl.BlockSpec(
            (MEM_DEV, 2 * PER_STEP, 8, 512), lambda i: (0, base + i, 0, 0)
        ),
        scratch_shapes=[pltpu.VMEM((8 * PER_STEP, 64, LANES), jnp.float32)],
        input_output_aliases=aliases,
        compiler_params=pltpu.CompilerParams(vmem_limit_bytes=VMEM_LIMIT),
        cost_estimate=relayout_cost(count),
        name="unpack",
    )(*operands)


def gather_kernel(counts, tiles, info_ref, *refs):
    blocks, o_ref, held = refs[: len(counts)], refs[-2], refs[-1]
    step = pl.program_id(0)
    lane_index = lax.broadcasted_iota(jnp.int32, (LANES, 256), 0)
    for t in range(tiles):
        a = step * tiles + t
        info = info_ref[a]
        cell = info[0:1].astype(jnp.int32)
        channel = info[1:2].astype(jnp.int32)
        lane = (channel & 1) * 64 + (cell & 63)
        group = (channel >> 1) * 2 + (cell >> 6)
        pick = (lane_index == lane).astype(jnp.float32).astype(jnp.bfloat16)
        total = jnp.zeros((MEM_DEV, 256), jnp.float32)
        first = 0
        for block, count in zip(blocks, counts):
            rows = block[t, :count].reshape(count * 16, LANES)
            found = lax.dot_general(rows, pick, NN, preferred_element_type=jnp.float32)
            found = found.reshape(count * 2, MEM_DEV, 256)
            for g in range(count * 2):
                total = total + jnp.where(group == first * 2 + g, found[g], 0.0)
            first += count
        for half in range(2):
            part = total[:, half * LANES : (half + 1) * LANES]
            rows = pl.ds(half * 8, 8)
            held[lax.rem(a + 1, 32), 0, rows] = part
            held[a, 1, rows] = part
            held[lax.rem(a + 31, 32), 2, rows] = part

    @pl.when(step == 32 // tiles - 1)
    def _():
        o_ref[...] = held[...].astype(jnp.bfloat16)


def gather_obs(info, blocks):
    tiles = 4
    carrier = blocks[CARRIER]
    place = CHUNKS[CARRIER] // 3
    return pl.pallas_call(
        functools.partial(gather_kernel, CHUNKS, tiles),
        out_shape=jax.ShapeDtypeStruct(carrier.shape, jnp.bfloat16),
        grid=(32 // tiles,),
        in_specs=[pl.BlockSpec((32, 4, 256), lambda i: (0, 0, 0))]
        + [pl.BlockSpec((tiles,) + b.shape[1:], lambda i: (i, 0, 0, 0)) for b in blocks],
        out_specs=pl.BlockSpec((32, 3, 16, LANES), lambda i: (0, place, 0, 0)),
        scratch_shapes=[pltpu.VMEM((32, 3, 16, LANES), jnp.float32)],
        input_output_aliases={1 + CARRIER: 0},
        compiler_params=pltpu.CompilerParams(vmem_limit_bytes=VMEM_LIMIT),
        cost_estimate=pl.CostEstimate(
            flops=2 * 32 * 640 * 256 * 128, bytes_accessed=6 << 20, transcendentals=0
        ),
        name="gather_obs",
    )(info, *blocks)


def split(x):
    high = x.astype(jnp.bfloat16)
    return high, (x - high.astype(jnp.float32)).astype(jnp.bfloat16)


def product(a, b, dims):
    a_high, a_low = a if isinstance(a, tuple) else split(a)
    b_high, b_low = b if isinstance(b, tuple) else split(b)
    dot = functools.partial(
        lax.dot_general, dimension_numbers=dims, preferred_element_type=jnp.float32
    )
    return dot(a_high, b_high) + (dot(a_high, b_low) + dot(a_low, b_high))


def weights_kernel(own, below, above, own_info, below_info, above_info, w_ref, keep_ref, gram):
    members = 256
    row_id = lax.broadcasted_iota(jnp.int32, (members, members), 0)
    col_id = lax.broadcasted_iota(jnp.int32, (members, members), 1)
    identity = (row_id == col_id).astype(jnp.float32)
    drive = [jnp.zeros((8, members), jnp.float32) for _ in range(2)]
    first = True
    lon_centre = (LON_DEV - 1) / 2.0
    for j, (values, infos) in enumerate(
        ((below, below_info), (own, own_info), (above, above_info))
    ):
        lat_shift = (j - 1.0) * LAT_DEV
        for i in range(3):
            lon_shift = (i - 1.0) * LON_DEV
            halves = values[:, i].astype(jnp.float32).reshape(32, 2, MEM_DEV, LANES)
            hx = jnp.concatenate(
                [halves[:, half].reshape(members, LANES) for half in range(2)], axis=1
            )
            centre = jnp.sum(hx, axis=0, keepdims=True) * (1.0 / members)
            y = hx - centre
            y_parts = split(y)
            info = infos[i]
            cell = info[0:1].astype(jnp.int32)
            departure = info[2:3] - centre
            weight = info[3:4]
            lat = (cell >> 4).astype(jnp.float32) + lat_shift
            lon = (cell & 15).astype(jnp.float32) + lon_shift
            for p in range(2):
                lat_centre = p * PATCH_LAT + (PATCH_LAT - 1) / 2.0
                dist = (lat - lat_centre) ** 2 + (lon - lon_centre) ** 2
                obs_weight = jnp.exp(-dist / (2.0 * LOC * LOC)) * weight
                term = product(y * obs_weight, y_parts, NT)
                if first:
                    gram[p] = identity + term
                else:
                    gram[p] += term
                pull = jnp.broadcast_to(obs_weight * departure, (8, 256))
                drive[p] = drive[p] + product(pull, y_parts, NT)
            first = False
    roots, inverses, scales = [], [], []
    for p in range(2):
        system = gram[p]
        scale = jnp.sqrt(jnp.sum(jnp.sum(system * system, axis=0, keepdims=True), axis=1, keepdims=True))
        roots.append(system / scale)
        scales.append(scale)
    for step in range(NS_ITERS):
        for p in range(2):
            if step == 0:
                factor = 1.5 * identity - 0.5 * roots[p]
                f_parts = split(factor)
                roots[p] = product(roots[p], f_parts, NN)
                inverses_p = factor
                if len(inverses) < 2:
                    inverses.append(inverses_p)
            else:
                i_parts = split(inverses[p])
                r_parts = split(roots[p])
                factor = 1.5 * identity - 0.5 * product(i_parts, r_parts, NN)
                f_parts = split(factor)
                if step < NS_ITERS - 1:
                    roots[p] = product(r_parts, f_parts, NN)
                inverses[p] = product(f_parts, i_parts, NN)
    for p in range(2):
        spread = inverses[p] / jnp.sqrt(scales[p])
        s_parts = split(spread)
        shift = product(product(drive[p], s_parts, NT), s_parts, NT)
        weights = (spread + shift[0:1]).astype(jnp.bfloat16)
        w_ref[p] = weights
        total = jnp.sum(weights.astype(jnp.float32), axis=1, keepdims=True)
        keep_ref[p] = jnp.broadcast_to(1.0 - total, (members, LANES))


def tile_weights(values, infos):
    place = CHUNKS[CARRIER] // 3
    return pl.pallas_call(
        weights_kernel,
        out_shape=(
            jax.ShapeDtypeStruct((2, 256, 256), jnp.bfloat16),
            jax.ShapeDtypeStruct((2, 256, LANES), jnp.float32),
        ),
        grid=(1,),
        in_specs=[
            pl.BlockSpec((32, 3, 16, LANES), lambda i: (0, place, 0, 0)),
            pl.BlockSpec((32, 3, 16, LANES), lambda i: (0, 0, 0, 0)),
            pl.BlockSpec((32, 3, 16, LANES), lambda i: (0, 0, 0, 0)),
        ]
        + [pl.BlockSpec((3, 4, 256), lambda i: (0, 0, 0))] * 3,
        out_specs=(
            pl.BlockSpec((2, 256, 256), lambda i: (0, 0, 0)),
            pl.BlockSpec((2, 256, LANES), lambda i: (0, 0, 0)),
        ),
        scratch_shapes=[pltpu.VMEM((2, 256, 256), jnp.float32)],
        compiler_params=pltpu.CompilerParams(vmem_limit_bytes=VMEM_LIMIT),
        cost_estimate=pl.CostEstimate(
            flops=2 * 160 * 256**3, bytes_accessed=3 << 20, transcendentals=0
        ),
        name="tile_weights",
    )(*values, *infos)


def transform_kernel(per_step, x_ref, w_ref, keep_ref, *rest):
    o_ref = rest[-1]
    for b in range(per_step):
        both = x_ref[:, b].astype(jnp.float32).reshape(32, 2, MEM_DEV, LANES)
        outs = []
        for p in range(2):
            states = both[:, p].reshape(256, LANES)
            mean = jnp.sum(states, axis=0, keepdims=True) * (1.0 / 256.0)
            mixed = lax.dot_general(
                w_ref[p], states.astype(jnp.bfloat16), NN, preferred_element_type=jnp.float32
            )
            result = mixed + keep_ref[p] * mean
            outs.append(result.reshape(32, 1, MEM_DEV, LANES))
        result = jnp.concatenate(outs, axis=1).reshape(32, 16, LANES)
        o_ref[:, b] = result.astype(jnp.bfloat16)


def transform(blocks, count, weights, keep, per_step, total, first=0, previous=()):
    base = first // per_step
    spec = pl.BlockSpec((32, per_step, 16, LANES), lambda i: (0, i, 0, 0))
    return pl.pallas_call(
        functools.partial(transform_kernel, per_step),
        out_shape=jax.ShapeDtypeStruct((32, total, 16, LANES), jnp.bfloat16),
        grid=(count // per_step,),
        in_specs=[
            spec,
            pl.BlockSpec((2, 256, 256), lambda i: (0, 0, 0)),
            pl.BlockSpec((2, 256, LANES), lambda i: (0, 0, 0)),
        ]
        + [pl.BlockSpec(memory_space=pl.ANY)] * len(previous),
        out_specs=pl.BlockSpec((32, per_step, 16, LANES), lambda i: (0, base + i, 0, 0)),
        input_output_aliases={3: 0} if previous else {},
        compiler_params=pltpu.CompilerParams(vmem_limit_bytes=VMEM_LIMIT),
        cost_estimate=pl.CostEstimate(
            flops=count * 4 * 256 * 256 * 128, bytes_accessed=count * 262144, transcendentals=0
        ),
        name="transform",
    )(blocks, weights, keep, *previous)


def exchange(blocks):
    return lax.all_to_all(blocks, "member", split_axis=0, concat_axis=0, tiled=True)


def per_device(background, obs_cell, obs_channel, obs_count, obs_value, obs_precision):
    slots = obs_cell.shape[-1]
    members = 256
    inside = (jnp.arange(slots, dtype=jnp.int32) < obs_count[0, 0]).astype(jnp.float32)
    weight = inside * obs_precision[0, 0] / (members - 1.0)
    own = jnp.stack(
        [
            obs_cell[0, 0].astype(jnp.float32),
            obs_channel[0, 0].astype(jnp.float32),
            obs_value[0, 0],
            weight,
        ]
    )
    info = exchange(jnp.broadcast_to(own[None], (32,) + own.shape))
    parity = (1 - (lax.axis_index("tile") & 1)).astype(jnp.int32).reshape(1)
    (lead,) = pack(0, parity, background, (2,))
    lead, *rest = pack(1, parity, background, (2, 0, 1), (lead,), (info,))
    rest = pack(0, parity, background, (0, 1), tuple(rest), (lead,))
    blocks = [rest[0], rest[1], lead]
    blocks[CARRIER] = gather_obs(info, blocks)
    arrived = [exchange(b) for b in blocks]
    hx = arrived[CARRIER][:, CHUNKS[CARRIER] :]
    me = lax.axis_index("member")
    near = jnp.stack(
        [
            lax.dynamic_index_in_dim(info, lax.rem(me + d, 32), 0, keepdims=False)
            for d in (31, 0, 1)
        ]
    )
    bands = lax.axis_size("tile")
    up = [(i, i + 1) for i in range(bands - 1)]
    down = [(i + 1, i) for i in range(bands - 1)]
    values = (arrived[CARRIER], lax.ppermute(hx, "tile", up), lax.ppermute(hx, "tile", down))
    infos = (near, lax.ppermute(near, "tile", up), lax.ppermute(near, "tile", down))
    weights, keep = tile_weights(values, infos)

    total = CHUNKS[1] + CHUNKS[2]
    early = transform(arrived[2], CHUNKS[2], weights, keep, 4, total, CHUNKS[1])
    early = transform(arrived[1], CHUNKS[1], weights, keep, 4, total, 0, (early,))
    late = transform(arrived[0], CHUNKS[0], weights, keep, 4, CHUNKS[0])
    out = unpack(exchange(early), None, CHUNKS[0], total, background.shape)
    return unpack(exchange(late), out, 0, CHUNKS[0], background.shape)


def solution(mesh):
    in_specs = (
        P("member", None, "tile", None),
        P("member", "tile", None),
        P("member", "tile", None),
        P("member", "tile"),
        P("member", "tile", None),
        P("member", "tile", None),
    )
    out_specs = P("member", None, "tile", None)
    mapped = jax.shard_map(
        per_device, mesh=mesh, in_specs=in_specs, out_specs=out_specs, check_vma=False
    )

    def run(*args):
        with jax.sharding.use_abstract_mesh(mesh.abstract_mesh):
            return mapped(*args)

    return run
```

```python
import functools

import jax
import jax.numpy as jnp
from jax import lax
from jax.experimental import pallas as pl
from jax.experimental.pallas import tpu as pltpu
from jax.sharding import PartitionSpec as P

LAT_DEV = 8
LON_DEV = 16
PATCH_LAT = 4
NS_ITERS = 6
LOC = 8
MEM_DEV = 8
LANES = 128
CHUNKS = (20, 12, 8)
CARRIER = 1
PER_STEP = 4
NT = (((1,), (1,)), ((), ()))
NN = (((1,), (0,)), ((), ()))
VMEM_LIMIT = 48 * 1024 * 1024


def swap_groups(parts):
    lane_group = lax.broadcasted_iota(jnp.int32, parts[0].shape, 1) // LON_DEV
    parts = list(parts)
    for step in (4, 2, 1):
        low = (lane_group & step) == 0
        for i in range(8):
            if i & step:
                continue
            a, b = parts[i], parts[i + step]
            if step == 4:
                crossed = pltpu.roll(jnp.where(low, b, a), 64, 1)
                parts[i] = jnp.where(low, a, crossed)
                parts[i + step] = jnp.where(low, crossed, b)
            else:
                parts[i] = jnp.where(low, a, pltpu.roll(b, step * LON_DEV, 1))
                parts[i + step] = jnp.where(low, pltpu.roll(a, LANES - step * LON_DEV, 1), b)
    return parts


def lanes_of(g):
    return pl.ds(pl.multiple_of(g * LANES, LANES), LANES)


def pack_block(per_step, held, x_ref, o_ref):
    def unit(t, carry):
        b, g = t // 4, t % 4
        for e in range(2):
            cells = x_ref[:, b * 2 + e, :, lanes_of(g)].astype(jnp.float32)
            held[t * 2 + e] = cells.reshape(64, LANES)
        parts = []
        for e in range(2):
            for r in range(PATCH_LAT):
                halves = [
                    held[t * 2 + e, pl.ds(p * PATCH_LAT + r, MEM_DEV, stride=8), :]
                    for p in range(2)
                ]
                parts.append(jnp.concatenate(halves, axis=0).astype(jnp.bfloat16))
        for a, part in enumerate(swap_groups(parts)):
            o_ref[g * 8 + a, b] = part
        return carry

    lax.fori_loop(0, per_step * 4, unit, 0, unroll=8)


def pack_kernel(turn, ranges, parity_ref, x_ref, *refs):
    outs, held = refs[-1 - len(ranges) : -1], refs[-1]

    @pl.when(parity_ref[0] == turn)
    def _():
        for (first, count), o_ref in zip(ranges, outs):
            base = first // PER_STEP
            pltpu.emit_pipeline(
                functools.partial(pack_block, PER_STEP, held),
                grid=(count // PER_STEP,),
                in_specs=[
                    pl.BlockSpec(
                        (MEM_DEV, 2 * PER_STEP, 8, 512), lambda i, base=base: (0, base + i, 0, 0)
                    )
                ],
                out_specs=[pl.BlockSpec((32, PER_STEP, 16, LANES), lambda i: (0, i, 0, 0))],
            )(x_ref, o_ref)


def pack(turn, parity, background, chunks, previous=(), after=()):
    anywhere = pl.BlockSpec(memory_space=pl.ANY)
    firsts = [sum(CHUNKS[:n]) for n in chunks]
    ranges = tuple((f, CHUNKS[n]) for f, n in zip(firsts, chunks))
    return pl.pallas_call(
        functools.partial(pack_kernel, turn, ranges),
        out_shape=tuple(
            jax.ShapeDtypeStruct(
                (32, CHUNKS[n] + (3 if n == CARRIER else 0), 16, LANES), jnp.bfloat16
            )
            for n in chunks
        ),
        in_specs=[pl.BlockSpec(memory_space=pltpu.SMEM), anywhere]
        + [anywhere] * (len(previous) + len(after)),
        out_specs=(anywhere,) * len(chunks),
        scratch_shapes=[pltpu.VMEM((8 * PER_STEP, 64, LANES), jnp.float32)],
        input_output_aliases={2 + n: n for n in range(len(previous))},
        compiler_params=pltpu.CompilerParams(vmem_limit_bytes=VMEM_LIMIT),
        cost_estimate=relayout_cost(sum(count for _, count in ranges)),
        name="pack",
    )(parity, background, *previous, *after)


def relayout_cost(count):
    return pl.CostEstimate(
        flops=count * 65536 * 40, bytes_accessed=count * 262144, transcendentals=0
    )


def unpack_kernel(per_step, x_ref, *rest):
    o_ref, held = rest[-2:]

    def unit(t, carry):
        b, g = t // 4, t % 4
        parts = swap_groups([x_ref[g * 8 + a, b] for a in range(8)])
        for e in range(2):
            for r in range(PATCH_LAT):
                both = parts[e * PATCH_LAT + r].astype(jnp.float32)
                for p in range(2):
                    held[t * 2 + e, pl.ds(p * PATCH_LAT + r, MEM_DEV, stride=8), :] = both[
                        p * 8 : (p + 1) * 8
                    ]
        for e in range(2):
            cells = held[t * 2 + e].reshape(MEM_DEV, 8, LANES)
            o_ref[:, b * 2 + e, :, lanes_of(g)] = cells.astype(jnp.bfloat16)
        return carry

    lax.fori_loop(0, per_step * 4, unit, 0, unroll=8)


def unpack(blocks, previous, first, count, shape):
    base = first // PER_STEP
    in_specs = [pl.BlockSpec((32, PER_STEP, 16, LANES), lambda i: (0, i, 0, 0))]
    operands = [blocks]
    aliases = {}
    if previous is not None:
        in_specs.append(pl.BlockSpec(memory_space=pl.ANY))
        operands.append(previous)
        aliases = {1: 0}
    return pl.pallas_call(
        functools.partial(unpack_kernel, PER_STEP),
        out_shape=jax.ShapeDtypeStruct(shape, jnp.bfloat16),
        grid=(count // PER_STEP,),
        in_specs=in_specs,
        out_specs=pl.BlockSpec(
            (MEM_DEV, 2 * PER_STEP, 8, 512), lambda i: (0, base + i, 0, 0)
        ),
        scratch_shapes=[pltpu.VMEM((8 * PER_STEP, 64, LANES), jnp.float32)],
        input_output_aliases=aliases,
        compiler_params=pltpu.CompilerParams(vmem_limit_bytes=VMEM_LIMIT),
        cost_estimate=relayout_cost(count),
        name="unpack",
    )(*operands)


def gather_kernel(counts, tiles, info_ref, *refs):
    blocks, o_ref, held = refs[: len(counts)], refs[-2], refs[-1]
    step = pl.program_id(0)
    lane_index = lax.broadcasted_iota(jnp.int32, (LANES, 256), 0)
    for t in range(tiles):
        a = step * tiles + t
        info = info_ref[a]
        cell = info[0:1].astype(jnp.int32)
        channel = info[1:2].astype(jnp.int32)
        lane = (channel & 1) * 64 + (cell & 63)
        group = (channel >> 1) * 2 + (cell >> 6)
        pick = (lane_index == lane).astype(jnp.float32).astype(jnp.bfloat16)
        total = jnp.zeros((MEM_DEV, 256), jnp.float32)
        first = 0
        for block, count in zip(blocks, counts):
            rows = block[t, :count].reshape(count * 16, LANES)
            found = lax.dot_general(rows, pick, NN, preferred_element_type=jnp.float32)
            found = found.reshape(count * 2, MEM_DEV, 256)
            for g in range(count * 2):
                total = total + jnp.where(group == first * 2 + g, found[g], 0.0)
            first += count
        for half in range(2):
            part = total[:, half * LANES : (half + 1) * LANES]
            rows = pl.ds(half * 8, 8)
            held[lax.rem(a + 1, 32), 0, rows] = part
            held[a, 1, rows] = part
            held[lax.rem(a + 31, 32), 2, rows] = part

    @pl.when(step == 32 // tiles - 1)
    def _():
        o_ref[...] = held[...].astype(jnp.bfloat16)


def gather_obs(info, blocks):
    tiles = 4
    carrier = blocks[CARRIER]
    place = CHUNKS[CARRIER] // 3
    return pl.pallas_call(
        functools.partial(gather_kernel, CHUNKS, tiles),
        out_shape=jax.ShapeDtypeStruct(carrier.shape, jnp.bfloat16),
        grid=(32 // tiles,),
        in_specs=[pl.BlockSpec((32, 4, 256), lambda i: (0, 0, 0))]
        + [pl.BlockSpec((tiles,) + b.shape[1:], lambda i: (i, 0, 0, 0)) for b in blocks],
        out_specs=pl.BlockSpec((32, 3, 16, LANES), lambda i: (0, place, 0, 0)),
        scratch_shapes=[pltpu.VMEM((32, 3, 16, LANES), jnp.float32)],
        input_output_aliases={1 + CARRIER: 0},
        compiler_params=pltpu.CompilerParams(vmem_limit_bytes=VMEM_LIMIT),
        cost_estimate=pl.CostEstimate(
            flops=2 * 32 * 640 * 256 * 128, bytes_accessed=6 << 20, transcendentals=0
        ),
        name="gather_obs",
    )(info, *blocks)


def split(x):
    high = x.astype(jnp.bfloat16)
    return high, (x - high.astype(jnp.float32)).astype(jnp.bfloat16)


def product(a, b, dims):
    a_high, a_low = a if isinstance(a, tuple) else split(a)
    b_high, b_low = b if isinstance(b, tuple) else split(b)
    dot = functools.partial(
        lax.dot_general, dimension_numbers=dims, preferred_element_type=jnp.float32
    )
    return dot(a_high, b_high) + (dot(a_high, b_low) + dot(a_low, b_high))


def weights_kernel(own, below, above, own_info, below_info, above_info, w_ref, keep_ref, gram):
    members = 256
    row_id = lax.broadcasted_iota(jnp.int32, (members, members), 0)
    col_id = lax.broadcasted_iota(jnp.int32, (members, members), 1)
    identity = (row_id == col_id).astype(jnp.float32)
    drive = [jnp.zeros((8, members), jnp.float32) for _ in range(2)]
    first = True
    lon_centre = (LON_DEV - 1) / 2.0
    for j, (values, infos) in enumerate(
        ((below, below_info), (own, own_info), (above, above_info))
    ):
        lat_shift = (j - 1.0) * LAT_DEV
        for i in range(3):
            lon_shift = (i - 1.0) * LON_DEV
            halves = values[:, i].astype(jnp.float32).reshape(32, 2, MEM_DEV, LANES)
            hx = jnp.concatenate(
                [halves[:, half].reshape(members, LANES) for half in range(2)], axis=1
            )
            centre = jnp.sum(hx, axis=0, keepdims=True) * (1.0 / members)
            y = hx - centre
            y_parts = split(y)
            info = infos[i]
            cell = info[0:1].astype(jnp.int32)
            departure = info[2:3] - centre
            weight = info[3:4]
            lat = (cell >> 4).astype(jnp.float32) + lat_shift
            lon = (cell & 15).astype(jnp.float32) + lon_shift
            for p in range(2):
                lat_centre = p * PATCH_LAT + (PATCH_LAT - 1) / 2.0
                dist = (lat - lat_centre) ** 2 + (lon - lon_centre) ** 2
                obs_weight = jnp.exp(-dist / (2.0 * LOC * LOC)) * weight
                term = product(y * obs_weight, y_parts, NT)
                if first:
                    gram[p] = identity + term
                else:
                    gram[p] += term
                pull = jnp.broadcast_to(obs_weight * departure, (8, 256))
                drive[p] = drive[p] + product(pull, y_parts, NT)
            first = False
    roots, inverses, scales = [], [], []
    for p in range(2):
        system = gram[p]
        scale = jnp.sqrt(jnp.sum(jnp.sum(system * system, axis=0, keepdims=True), axis=1, keepdims=True))
        roots.append(system / scale)
        scales.append(scale)
    for step in range(NS_ITERS):
        for p in range(2):
            if step == 0:
                factor = 1.5 * identity - 0.5 * roots[p]
                f_parts = split(factor)
                roots[p] = product(roots[p], f_parts, NN)
                inverses_p = factor
                if len(inverses) < 2:
                    inverses.append(inverses_p)
            else:
                i_parts = split(inverses[p])
                r_parts = split(roots[p])
                factor = 1.5 * identity - 0.5 * product(i_parts, r_parts, NN)
                f_parts = split(factor)
                if step < NS_ITERS - 1:
                    roots[p] = product(r_parts, f_parts, NN)
                inverses[p] = product(f_parts, i_parts, NN)
    for p in range(2):
        spread = inverses[p] / jnp.sqrt(scales[p])
        s_parts = split(spread)
        shift = product(product(drive[p], s_parts, NT), s_parts, NT)
        weights = (spread + shift[0:1]).astype(jnp.bfloat16)
        w_ref[p] = weights
        total = jnp.sum(weights.astype(jnp.float32), axis=1, keepdims=True)
        keep_ref[p] = jnp.broadcast_to(1.0 - total, (members, LANES))


def tile_weights(values, infos):
    place = CHUNKS[CARRIER] // 3
    return pl.pallas_call(
        weights_kernel,
        out_shape=(
            jax.ShapeDtypeStruct((2, 256, 256), jnp.bfloat16),
            jax.ShapeDtypeStruct((2, 256, LANES), jnp.float32),
        ),
        grid=(1,),
        in_specs=[
            pl.BlockSpec((32, 3, 16, LANES), lambda i: (0, place, 0, 0)),
            pl.BlockSpec((32, 3, 16, LANES), lambda i: (0, 0, 0, 0)),
            pl.BlockSpec((32, 3, 16, LANES), lambda i: (0, 0, 0, 0)),
        ]
        + [pl.BlockSpec((3, 4, 256), lambda i: (0, 0, 0))] * 3,
        out_specs=(
            pl.BlockSpec((2, 256, 256), lambda i: (0, 0, 0)),
            pl.BlockSpec((2, 256, LANES), lambda i: (0, 0, 0)),
        ),
        scratch_shapes=[pltpu.VMEM((2, 256, 256), jnp.float32)],
        compiler_params=pltpu.CompilerParams(vmem_limit_bytes=VMEM_LIMIT),
        cost_estimate=pl.CostEstimate(
            flops=2 * 160 * 256**3, bytes_accessed=3 << 20, transcendentals=0
        ),
        name="tile_weights",
    )(*values, *infos)


def transform_kernel(per_step, x_ref, w_ref, keep_ref, *rest):
    o_ref = rest[-1]
    for b in range(per_step):
        both = x_ref[:, b].astype(jnp.float32).reshape(32, 2, MEM_DEV, LANES)
        outs = []
        for p in range(2):
            states = both[:, p].reshape(256, LANES)
            mean = jnp.sum(states, axis=0, keepdims=True) * (1.0 / 256.0)
            mixed = lax.dot_general(
                w_ref[p], states.astype(jnp.bfloat16), NN, preferred_element_type=jnp.float32
            )
            result = mixed + keep_ref[p] * mean
            outs.append(result.reshape(32, 1, MEM_DEV, LANES))
        result = jnp.concatenate(outs, axis=1).reshape(32, 16, LANES)
        o_ref[:, b] = result.astype(jnp.bfloat16)


def transform(blocks, count, weights, keep, per_step, total, first=0, previous=()):
    base = first // per_step
    spec = pl.BlockSpec((32, per_step, 16, LANES), lambda i: (0, i, 0, 0))
    return pl.pallas_call(
        functools.partial(transform_kernel, per_step),
        out_shape=jax.ShapeDtypeStruct((32, total, 16, LANES), jnp.bfloat16),
        grid=(count // per_step,),
        in_specs=[
            spec,
            pl.BlockSpec((2, 256, 256), lambda i: (0, 0, 0)),
            pl.BlockSpec((2, 256, LANES), lambda i: (0, 0, 0)),
        ]
        + [pl.BlockSpec(memory_space=pl.ANY)] * len(previous),
        out_specs=pl.BlockSpec((32, per_step, 16, LANES), lambda i: (0, base + i, 0, 0)),
        input_output_aliases={3: 0} if previous else {},
        compiler_params=pltpu.CompilerParams(vmem_limit_bytes=VMEM_LIMIT),
        cost_estimate=pl.CostEstimate(
            flops=count * 4 * 256 * 256 * 128, bytes_accessed=count * 262144, transcendentals=0
        ),
        name="transform",
    )(blocks, weights, keep, *previous)


def slot_rows_kernel(count_ref, cell_ref, channel_ref, value_ref, precision_ref, o_ref):
    shape = (1, 256)
    inside = lax.broadcasted_iota(jnp.int32, shape, 1) < count_ref[0, 0]
    weight = inside.astype(jnp.float32) * precision_ref[0] / 255.0
    rows = (
        cell_ref[0].astype(jnp.float32),
        channel_ref[0].astype(jnp.float32),
        value_ref[0],
        weight,
    )
    for n, row in enumerate(rows):
        o_ref[:, n : n + 1] = jnp.broadcast_to(row[None], (32, 1, 256))


def slot_rows(count, *rows):
    vmem = pl.BlockSpec(memory_space=pltpu.VMEM)
    return pl.pallas_call(
        slot_rows_kernel,
        out_shape=jax.ShapeDtypeStruct((32, 4, 256), jnp.float32),
        in_specs=[pl.BlockSpec(memory_space=pltpu.SMEM)] + [vmem] * 4,
        out_specs=vmem,
        name="slot_rows",
    )(count, *rows)


def exchange(blocks):
    return lax.all_to_all(blocks, "member", split_axis=0, concat_axis=0, tiled=True)


def per_device(background, obs_cell, obs_channel, obs_count, obs_value, obs_precision):
    info = exchange(
        slot_rows(obs_count, obs_cell, obs_channel, obs_value, obs_precision)
    )
    parity = (1 - (lax.axis_index("tile") & 1)).astype(jnp.int32).reshape(1)
    (lead,) = pack(0, parity, background, (2,))
    lead, *rest = pack(1, parity, background, (2, 0, 1), (lead,), (info,))
    rest = pack(0, parity, background, (0, 1), tuple(rest), (lead,))
    blocks = [rest[0], rest[1], lead]
    blocks[CARRIER] = gather_obs(info, blocks)
    arrived = [exchange(b) for b in blocks]
    hx = arrived[CARRIER][:, CHUNKS[CARRIER] :]
    me = lax.axis_index("member")
    near = jnp.stack(
        [
            lax.dynamic_index_in_dim(info, lax.rem(me + d, 32), 0, keepdims=False)
            for d in (31, 0, 1)
        ]
    )
    bands = lax.axis_size("tile")
    up = [(i, i + 1) for i in range(bands - 1)]
    down = [(i + 1, i) for i in range(bands - 1)]
    values = (arrived[CARRIER], lax.ppermute(hx, "tile", up), lax.ppermute(hx, "tile", down))
    infos = (near, lax.ppermute(near, "tile", up), lax.ppermute(near, "tile", down))
    weights, keep = tile_weights(values, infos)

    total = CHUNKS[1] + CHUNKS[2]
    early = transform(arrived[2], CHUNKS[2], weights, keep, 4, total, CHUNKS[1])
    early = transform(arrived[1], CHUNKS[1], weights, keep, 4, total, 0, (early,))
    late = transform(arrived[0], CHUNKS[0], weights, keep, 4, CHUNKS[0])
    out = unpack(exchange(early), None, CHUNKS[0], total, background.shape)
    return unpack(exchange(late), out, 0, CHUNKS[0], background.shape)


def solution(mesh):
    in_specs = (
        P("member", None, "tile", None),
        P("member", "tile", None),
        P("member", "tile", None),
        P("member", "tile"),
        P("member", "tile", None),
        P("member", "tile", None),
    )
    out_specs = P("member", None, "tile", None)
    mapped = jax.shard_map(
        per_device, mesh=mesh, in_specs=in_specs, out_specs=out_specs, check_vma=False
    )

    def run(*args):
        with jax.sharding.use_abstract_mesh(mesh.abstract_mesh):
            return mapped(*args)

    return run
```

```python
import functools

import jax
import jax.numpy as jnp
from jax import lax
from jax.experimental import pallas as pl
from jax.experimental.pallas import tpu as pltpu
from jax.sharding import PartitionSpec as P

LAT_DEV = 8
LON_DEV = 16
PATCH_LAT = 4
NS_ITERS = 6
LOC = 8
MEM_DEV = 8
LANES = 128
CHUNKS = (20, 12, 8)
CARRIER = 1
PER_STEP = 4
NT = (((1,), (1,)), ((), ()))
NN = (((1,), (0,)), ((), ()))
VMEM_LIMIT = 48 * 1024 * 1024


def swap_groups(parts):
    lane_group = lax.broadcasted_iota(jnp.int32, parts[0].shape, 1) // LON_DEV
    parts = list(parts)
    for step in (4, 2, 1):
        low = (lane_group & step) == 0
        for i in range(8):
            if i & step:
                continue
            a, b = parts[i], parts[i + step]
            if step == 4:
                crossed = pltpu.roll(jnp.where(low, b, a), 64, 1)
                parts[i] = jnp.where(low, a, crossed)
                parts[i + step] = jnp.where(low, crossed, b)
            else:
                parts[i] = jnp.where(low, a, pltpu.roll(b, step * LON_DEV, 1))
                parts[i + step] = jnp.where(low, pltpu.roll(a, LANES - step * LON_DEV, 1), b)
    return parts


def lanes_of(g):
    return pl.ds(pl.multiple_of(g * LANES, LANES), LANES)


def pack_block(per_step, held, x_ref, o_ref):
    def unit(t, carry):
        b, g = t // 4, t % 4
        for e in range(2):
            cells = x_ref[:, b * 2 + e, :, lanes_of(g)].astype(jnp.float32)
            held[t * 2 + e] = cells.reshape(64, LANES)
        parts = []
        for e in range(2):
            for r in range(PATCH_LAT):
                halves = [
                    held[t * 2 + e, pl.ds(p * PATCH_LAT + r, MEM_DEV, stride=8), :]
                    for p in range(2)
                ]
                parts.append(jnp.concatenate(halves, axis=0).astype(jnp.bfloat16))
        for a, part in enumerate(swap_groups(parts)):
            o_ref[g * 8 + a, b] = part
        return carry

    lax.fori_loop(0, per_step * 4, unit, 0, unroll=8)


def pack_kernel(turn, ranges, parity_ref, x_ref, *refs):
    outs, held = refs[-1 - len(ranges) : -1], refs[-1]

    @pl.when(parity_ref[0] == turn)
    def _():
        for (first, count), o_ref in zip(ranges, outs):
            base = first // PER_STEP
            pltpu.emit_pipeline(
                functools.partial(pack_block, PER_STEP, held),
                grid=(count // PER_STEP,),
                in_specs=[
                    pl.BlockSpec(
                        (MEM_DEV, 2 * PER_STEP, 8, 512), lambda i, base=base: (0, base + i, 0, 0)
                    )
                ],
                out_specs=[pl.BlockSpec((32, PER_STEP, 16, LANES), lambda i: (0, i, 0, 0))],
            )(x_ref, o_ref)


def pack(turn, parity, background, chunks, previous=(), after=()):
    anywhere = pl.BlockSpec(memory_space=pl.ANY)
    firsts = [sum(CHUNKS[:n]) for n in chunks]
    ranges = tuple((f, CHUNKS[n]) for f, n in zip(firsts, chunks))
    return pl.pallas_call(
        functools.partial(pack_kernel, turn, ranges),
        out_shape=tuple(
            jax.ShapeDtypeStruct(
                (32, CHUNKS[n] + (3 if n == CARRIER else 0), 16, LANES), jnp.bfloat16
            )
            for n in chunks
        ),
        in_specs=[pl.BlockSpec(memory_space=pltpu.SMEM), anywhere]
        + [anywhere] * (len(previous) + len(after)),
        out_specs=(anywhere,) * len(chunks),
        scratch_shapes=[pltpu.VMEM((8 * PER_STEP, 64, LANES), jnp.float32)],
        input_output_aliases={2 + n: n for n in range(len(previous))},
        compiler_params=pltpu.CompilerParams(vmem_limit_bytes=VMEM_LIMIT),
        cost_estimate=relayout_cost(sum(count for _, count in ranges)),
        name="pack",
    )(parity, background, *previous, *after)


def relayout_cost(count):
    return pl.CostEstimate(
        flops=count * 65536 * 40, bytes_accessed=count * 262144, transcendentals=0
    )


def unpack_kernel(per_step, x_ref, *rest):
    o_ref, held = rest[-2:]

    def unit(t, carry):
        b, g = t // 4, t % 4
        parts = swap_groups([x_ref[g * 8 + a, b] for a in range(8)])
        for e in range(2):
            for r in range(PATCH_LAT):
                both = parts[e * PATCH_LAT + r].astype(jnp.float32)
                for p in range(2):
                    held[t * 2 + e, pl.ds(p * PATCH_LAT + r, MEM_DEV, stride=8), :] = both[
                        p * 8 : (p + 1) * 8
                    ]
        for e in range(2):
            cells = held[t * 2 + e].reshape(MEM_DEV, 8, LANES)
            o_ref[:, b * 2 + e, :, lanes_of(g)] = cells.astype(jnp.bfloat16)
        return carry

    lax.fori_loop(0, per_step * 4, unit, 0, unroll=8)


def unpack(blocks, previous, first, count, shape):
    base = first // PER_STEP
    in_specs = [pl.BlockSpec((32, PER_STEP, 16, LANES), lambda i: (0, i, 0, 0))]
    operands = [blocks]
    aliases = {}
    if previous is not None:
        in_specs.append(pl.BlockSpec(memory_space=pl.ANY))
        operands.append(previous)
        aliases = {1: 0}
    return pl.pallas_call(
        functools.partial(unpack_kernel, PER_STEP),
        out_shape=jax.ShapeDtypeStruct(shape, jnp.bfloat16),
        grid=(count // PER_STEP,),
        in_specs=in_specs,
        out_specs=pl.BlockSpec(
            (MEM_DEV, 2 * PER_STEP, 8, 512), lambda i: (0, base + i, 0, 0)
        ),
        scratch_shapes=[pltpu.VMEM((8 * PER_STEP, 64, LANES), jnp.float32)],
        input_output_aliases=aliases,
        compiler_params=pltpu.CompilerParams(vmem_limit_bytes=VMEM_LIMIT),
        cost_estimate=relayout_cost(count),
        name="unpack",
    )(*operands)


def gather_kernel(counts, tiles, info_ref, *refs):
    blocks, o_ref, held = refs[: len(counts)], refs[-2], refs[-1]
    step = pl.program_id(0)
    lane_index = lax.broadcasted_iota(jnp.int32, (LANES, 256), 0)
    for t in range(tiles):
        a = step * tiles + t
        info = info_ref[a]
        cell = info[0:1].astype(jnp.int32)
        channel = info[1:2].astype(jnp.int32)
        lane = (channel & 1) * 64 + (cell & 63)
        group = (channel >> 1) * 2 + (cell >> 6)
        pick = (lane_index == lane).astype(jnp.float32).astype(jnp.bfloat16)
        total = jnp.zeros((MEM_DEV, 256), jnp.float32)
        first = 0
        for block, count in zip(blocks, counts):
            rows = block[t, :count].reshape(count * 16, LANES)
            found = lax.dot_general(rows, pick, NN, preferred_element_type=jnp.float32)
            found = found.reshape(count * 2, MEM_DEV, 256)
            for g in range(count * 2):
                total = total + jnp.where(group == first * 2 + g, found[g], 0.0)
            first += count
        for half in range(2):
            part = total[:, half * LANES : (half + 1) * LANES]
            rows = pl.ds(half * 8, 8)
            held[lax.rem(a + 1, 32), 0, rows] = part
            held[a, 1, rows] = part
            held[lax.rem(a + 31, 32), 2, rows] = part

    @pl.when(step == 32 // tiles - 1)
    def _():
        o_ref[...] = held[...].astype(jnp.bfloat16)


def gather_obs(info, blocks):
    tiles = 4
    carrier = blocks[CARRIER]
    place = CHUNKS[CARRIER] // 3
    return pl.pallas_call(
        functools.partial(gather_kernel, CHUNKS, tiles),
        out_shape=jax.ShapeDtypeStruct(carrier.shape, jnp.bfloat16),
        grid=(32 // tiles,),
        in_specs=[pl.BlockSpec((32, 4, 256), lambda i: (0, 0, 0))]
        + [pl.BlockSpec((tiles,) + b.shape[1:], lambda i: (i, 0, 0, 0)) for b in blocks],
        out_specs=pl.BlockSpec((32, 3, 16, LANES), lambda i: (0, place, 0, 0)),
        scratch_shapes=[pltpu.VMEM((32, 3, 16, LANES), jnp.float32)],
        input_output_aliases={1 + CARRIER: 0},
        compiler_params=pltpu.CompilerParams(vmem_limit_bytes=VMEM_LIMIT),
        cost_estimate=pl.CostEstimate(
            flops=2 * 32 * 640 * 256 * 128, bytes_accessed=6 << 20, transcendentals=0
        ),
        name="gather_obs",
    )(info, *blocks)


def split(x):
    high = x.astype(jnp.bfloat16)
    return high, (x - high.astype(jnp.float32)).astype(jnp.bfloat16)


def product(a, b, dims):
    a_high, a_low = a if isinstance(a, tuple) else split(a)
    b_high, b_low = b if isinstance(b, tuple) else split(b)
    dot = functools.partial(
        lax.dot_general, dimension_numbers=dims, preferred_element_type=jnp.float32
    )
    return dot(a_high, b_high) + (dot(a_high, b_low) + dot(a_low, b_high))


def weights_kernel(own, below, above, own_info, below_info, above_info, w_ref, keep_ref, gram):
    members = 256
    row_id = lax.broadcasted_iota(jnp.int32, (members, members), 0)
    col_id = lax.broadcasted_iota(jnp.int32, (members, members), 1)
    identity = (row_id == col_id).astype(jnp.float32)
    drive = [jnp.zeros((8, members), jnp.float32) for _ in range(2)]
    first = True
    lon_centre = (LON_DEV - 1) / 2.0
    for j, (values, infos) in enumerate(
        ((below, below_info), (own, own_info), (above, above_info))
    ):
        lat_shift = (j - 1.0) * LAT_DEV
        for i in range(3):
            lon_shift = (i - 1.0) * LON_DEV
            halves = values[:, i].astype(jnp.float32).reshape(32, 2, MEM_DEV, LANES)
            hx = jnp.concatenate(
                [halves[:, half].reshape(members, LANES) for half in range(2)], axis=1
            )
            centre = jnp.sum(hx, axis=0, keepdims=True) * (1.0 / members)
            y = hx - centre
            y_parts = split(y)
            info = infos[i]
            cell = info[0:1].astype(jnp.int32)
            departure = info[2:3] - centre
            weight = info[3:4]
            lat = (cell >> 4).astype(jnp.float32) + lat_shift
            lon = (cell & 15).astype(jnp.float32) + lon_shift
            for p in range(2):
                lat_centre = p * PATCH_LAT + (PATCH_LAT - 1) / 2.0
                dist = (lat - lat_centre) ** 2 + (lon - lon_centre) ** 2
                obs_weight = jnp.exp(-dist / (2.0 * LOC * LOC)) * weight
                term = product(y * obs_weight, y_parts, NT)
                if first:
                    gram[p] = identity + term
                else:
                    gram[p] += term
                pull = jnp.broadcast_to(obs_weight * departure, (8, 256))
                drive[p] = drive[p] + product(pull, y_parts, NT)
            first = False
    roots, inverses, scales = [], [], []
    for p in range(2):
        system = gram[p]
        scale = jnp.sqrt(jnp.sum(jnp.sum(system * system, axis=0, keepdims=True), axis=1, keepdims=True))
        roots.append(system / scale)
        scales.append(scale)
    for step in range(NS_ITERS):
        for p in range(2):
            if step == 0:
                factor = 1.5 * identity - 0.5 * roots[p]
                f_parts = split(factor)
                roots[p] = product(roots[p], f_parts, NN)
                inverses_p = factor
                if len(inverses) < 2:
                    inverses.append(inverses_p)
            else:
                i_parts = split(inverses[p])
                r_parts = split(roots[p])
                factor = 1.5 * identity - 0.5 * product(i_parts, r_parts, NN)
                f_parts = split(factor)
                if step < NS_ITERS - 1:
                    roots[p] = product(r_parts, f_parts, NN)
                inverses[p] = product(f_parts, i_parts, NN)
    for p in range(2):
        spread = inverses[p] / jnp.sqrt(scales[p])
        s_parts = split(spread)
        shift = product(product(drive[p], s_parts, NT), s_parts, NT)
        weights = (spread + shift[0:1]).astype(jnp.bfloat16)
        w_ref[p] = weights
        total = jnp.sum(weights.astype(jnp.float32), axis=1, keepdims=True)
        keep_ref[p] = jnp.broadcast_to(1.0 - total, (members, LANES))


def tile_weights(values, infos):
    place = CHUNKS[CARRIER] // 3
    return pl.pallas_call(
        weights_kernel,
        out_shape=(
            jax.ShapeDtypeStruct((2, 256, 256), jnp.bfloat16),
            jax.ShapeDtypeStruct((2, 256, LANES), jnp.float32),
        ),
        grid=(1,),
        in_specs=[
            pl.BlockSpec((32, 3, 16, LANES), lambda i: (0, place, 0, 0)),
            pl.BlockSpec((32, 3, 16, LANES), lambda i: (0, 0, 0, 0)),
            pl.BlockSpec((32, 3, 16, LANES), lambda i: (0, 0, 0, 0)),
        ]
        + [pl.BlockSpec((3, 4, 256), lambda i: (0, 0, 0))] * 3,
        out_specs=(
            pl.BlockSpec((2, 256, 256), lambda i: (0, 0, 0)),
            pl.BlockSpec((2, 256, LANES), lambda i: (0, 0, 0)),
        ),
        scratch_shapes=[pltpu.VMEM((2, 256, 256), jnp.float32)],
        compiler_params=pltpu.CompilerParams(vmem_limit_bytes=VMEM_LIMIT),
        cost_estimate=pl.CostEstimate(
            flops=2 * 160 * 256**3, bytes_accessed=3 << 20, transcendentals=0
        ),
        name="tile_weights",
    )(*values, *infos)


def transform_kernel(per_step, x_ref, w_ref, keep_ref, *rest):
    o_ref = rest[-1]
    for b in range(per_step):
        both = x_ref[:, b].astype(jnp.float32).reshape(32, 2, MEM_DEV, LANES)
        outs = []
        for p in range(2):
            states = both[:, p].reshape(256, LANES)
            mean = jnp.sum(states, axis=0, keepdims=True) * (1.0 / 256.0)
            mixed = lax.dot_general(
                w_ref[p], states.astype(jnp.bfloat16), NN, preferred_element_type=jnp.float32
            )
            result = mixed + keep_ref[p] * mean
            outs.append(result.reshape(32, 1, MEM_DEV, LANES))
        result = jnp.concatenate(outs, axis=1).reshape(32, 16, LANES)
        o_ref[:, b] = result.astype(jnp.bfloat16)


def transform(blocks, count, weights, keep, per_step, total, first=0, previous=()):
    base = first // per_step
    spec = pl.BlockSpec((32, per_step, 16, LANES), lambda i: (0, i, 0, 0))
    return pl.pallas_call(
        functools.partial(transform_kernel, per_step),
        out_shape=jax.ShapeDtypeStruct((32, total, 16, LANES), jnp.bfloat16),
        grid=(count // per_step,),
        in_specs=[
            spec,
            pl.BlockSpec((2, 256, 256), lambda i: (0, 0, 0)),
            pl.BlockSpec((2, 256, LANES), lambda i: (0, 0, 0)),
        ]
        + [pl.BlockSpec(memory_space=pl.ANY)] * len(previous),
        out_specs=pl.BlockSpec((32, per_step, 16, LANES), lambda i: (0, base + i, 0, 0)),
        input_output_aliases={3: 0} if previous else {},
        compiler_params=pltpu.CompilerParams(vmem_limit_bytes=VMEM_LIMIT),
        cost_estimate=pl.CostEstimate(
            flops=count * 4 * 256 * 256 * 128, bytes_accessed=count * 262144, transcendentals=0
        ),
        name="transform",
    )(blocks, weights, keep, *previous)


def slot_rows_kernel(count_ref, cell_ref, channel_ref, value_ref, precision_ref, o_ref):
    shape = (1, 256)
    inside = lax.broadcasted_iota(jnp.int32, shape, 1) < count_ref[0, 0]
    weight = inside.astype(jnp.float32) * precision_ref[0] / 255.0
    rows = (
        cell_ref[0].astype(jnp.float32),
        channel_ref[0].astype(jnp.float32),
        value_ref[0],
        weight,
    )
    for n, row in enumerate(rows):
        o_ref[:, n : n + 1] = jnp.broadcast_to(row[None], (32, 1, 256))


def slot_rows(count, *rows):
    vmem = pl.BlockSpec(memory_space=pltpu.VMEM)
    return pl.pallas_call(
        slot_rows_kernel,
        out_shape=jax.ShapeDtypeStruct((32, 4, 256), jnp.float32),
        in_specs=[pl.BlockSpec(memory_space=pltpu.SMEM)] + [vmem] * 4,
        out_specs=vmem,
        name="slot_rows",
    )(count, *rows)


def exchange(blocks):
    return lax.all_to_all(blocks, "member", split_axis=0, concat_axis=0, tiled=True)


def per_device(background, obs_cell, obs_channel, obs_count, obs_value, obs_precision):
    info = exchange(
        slot_rows(obs_count, obs_cell, obs_channel, obs_value, obs_precision)
    )
    parity = (1 - (lax.axis_index("tile") & 1)).astype(jnp.int32).reshape(1)
    lead, middle = pack(0, parity, background, (2, 1))
    lead, middle, longest = pack(
        1, parity, background, (2, 1, 0), (lead, middle), (info,)
    )
    (longest,) = pack(0, parity, background, (0,), (longest,), (lead,))
    rest = (longest, middle)
    blocks = [rest[0], rest[1], lead]
    blocks[CARRIER] = gather_obs(info, blocks)
    arrived = [exchange(b) for b in blocks]
    hx = arrived[CARRIER][:, CHUNKS[CARRIER] :]
    me = lax.axis_index("member")
    near = jnp.stack(
        [
            lax.dynamic_index_in_dim(info, lax.rem(me + d, 32), 0, keepdims=False)
            for d in (31, 0, 1)
        ]
    )
    bands = lax.axis_size("tile")
    up = [(i, i + 1) for i in range(bands - 1)]
    down = [(i + 1, i) for i in range(bands - 1)]
    values = (arrived[CARRIER], lax.ppermute(hx, "tile", up), lax.ppermute(hx, "tile", down))
    infos = (near, lax.ppermute(near, "tile", up), lax.ppermute(near, "tile", down))
    weights, keep = tile_weights(values, infos)

    total = CHUNKS[1] + CHUNKS[2]
    early = transform(arrived[2], CHUNKS[2], weights, keep, 4, total, CHUNKS[1])
    early = transform(arrived[1], CHUNKS[1], weights, keep, 4, total, 0, (early,))
    late = transform(arrived[0], CHUNKS[0], weights, keep, 4, CHUNKS[0])
    out = unpack(exchange(early), None, CHUNKS[0], total, background.shape)
    return unpack(exchange(late), out, 0, CHUNKS[0], background.shape)


def solution(mesh):
    in_specs = (
        P("member", None, "tile", None),
        P("member", "tile", None),
        P("member", "tile", None),
        P("member", "tile"),
        P("member", "tile", None),
        P("member", "tile", None),
    )
    out_specs = P("member", None, "tile", None)
    mapped = jax.shard_map(
        per_device, mesh=mesh, in_specs=in_specs, out_specs=out_specs, check_vma=False
    )

    def run(*args):
        with jax.sharding.use_abstract_mesh(mesh.abstract_mesh):
            return mapped(*args)

    return run
```
